512 devices in a mesh: row: 16 (over z_hi, y), col: 8 (over x, core), layer: 4 (over z_lo).
Axes of the slice: x: 4, y: 4, z: 16 (z_hi: 4, z_lo: 4; z = z_hi * 4 + z_lo), core: 2. Of those that a mesh axis runs over, the one named last changes fastest.
Arguments:
- a_vals: bfloat16 [8, 4, 2, 128, 4096], P('col', 'layer', None, 'row'), may hold values from -0.125 to 0.125
- a_pos: int32 [8, 4, 2, 128], P('col', 'layer', None, 'row'), may hold values from 0 to 128, as said below
- p_vals: bfloat16 [4, 2, 16, 64, 4096], P('layer', None, 'row', 'col'), may hold values from -6 to 6
- p_pos: int32 [4, 2, 16, 64], P('layer', None, 'row', 'col'), may hold values from 0 to 64, as said below
Outputs:
- galerkin: float32 [4096, 4096], P(('col', 'layer'), 'row')
The draws below stay inside these ranges and needn't reach their ends.
Inputs may be any that keep to these rules, and one draw needn't show every extreme that they name: `a_pos`: an entry below 128 is a block's place q in its panel (block row q // 16, block column q % 16); 128 marks an empty slot. No place repeats in a panel (the first three indices). In each aligned block of 8 slots the live ones come first; in every panel one run is full and every other run has an empty slot. `p_pos`: an entry below 64 is a block's place q in its panel (block row q // 4, block column q % 4); 64 marks an empty slot. No place repeats in a panel (the first three indices). In each aligned block of 8 slots the live ones come first; in every panel one run is full and every other run has an empty slot.
All inputs are finite; a program needn't handle non-finite values.
Results may differ from the reference program's by a relative error of at most 0.0003.
Values may be sent and summed in bfloat16 or wider, within the bound.
A program may use at most 64 MiB of HBM per device.

```python
import jax
import jax.numpy as jnp

BS = 64
RBC = 8
KBS = 16
CBR = 4
SECTIONS = 2
SLOTS_A = 8
SLOTS_P = 8
N_ROW = 16
N_COL = 8
N_LAYER = 4


def slot_places(key, panels, pieces, slots, span):
    keys = jax.random.split(key, 3)
    order = jax.vmap(lambda k: jax.random.permutation(k, span))(jax.random.split(keys[0], panels))
    order = order[:, :pieces * slots]
    counts = jax.random.randint(keys[1], (panels, pieces), 0, slots)
    full_piece = jax.random.randint(keys[2], (panels,), 0, pieces)
    counts = jnp.where(jnp.arange(pieces)[None, :] == full_piece[:, None], slots, counts)
    live = jnp.arange(slots)[None, None, :] < counts[:, :, None]
    return jnp.where(live.reshape(panels, pieces * slots), order, span).astype(jnp.int32)


def draw_a_pos(key, part):
    key = jax.random.fold_in(key, 11)
    places = slot_places(key, N_COL * N_LAYER * SECTIONS, N_ROW, SLOTS_A, RBC * KBS)
    return places.reshape(N_COL, N_LAYER, SECTIONS, N_ROW * SLOTS_A)


def draw_p_pos(key, part):
    key = jax.random.fold_in(key, 23)
    places = slot_places(key, N_LAYER * SECTIONS * N_ROW, N_COL, SLOTS_P, KBS * CBR)
    return places.reshape(N_LAYER, SECTIONS, N_ROW, N_COL * SLOTS_P)


def shard_levels(stream_key, shape, cuts, least, largest):
    gain, own = 1.0, jax.random.fold_in(stream_key, 6)
    for axis_at, blocks in cuts:
        draws = jnp.exp(jax.random.uniform(jax.random.fold_in(own, axis_at), (blocks,), jnp.float32, least / len(cuts), largest / len(cuts)))
        gain = gain * jnp.repeat(draws, shape[axis_at] // blocks).reshape([-1 if axis == axis_at else 1 for axis in range(len(shape))])
    return gain


def centred(rng, extent, scale, reach, cuts=(), kind=jnp.bfloat16):
    array = jax.random.normal(rng, extent, jnp.float32) * scale
    if len(cuts) > 0:
        array = shard_levels(rng, extent, cuts, -0.22, 0.18) * array
    return jnp.clip(array, min=-reach, max=reach).astype(kind)


def setup_inputs(seed: int = 0) -> dict:
    key_of = jax.random.split(jax.random.key(seed), 5)
    a_vals = centred(key_of[0], (N_COL, N_LAYER, SECTIONS, N_ROW * SLOTS_A, BS * BS), (2 * BS * KBS) ** -0.5, 0.125, ((0, 8), (1, 4), (3, 16)))
    a_pos = draw_a_pos(jax.random.fold_in(key_of[4], 71), 0)
    p_vals = centred(key_of[2], (N_LAYER, SECTIONS, N_ROW, N_COL * SLOTS_P, BS * BS), 1.0, 6.0, ((0, 4), (2, 16), (3, 8)))
    p_pos = draw_p_pos(jax.random.fold_in(key_of[4], 71), 0)
    return dict(a_vals=a_vals, a_pos=a_pos, p_vals=p_vals, p_pos=p_pos)


def densify(vals, pos, nrows, ncols):
    table = jnp.zeros((nrows * ncols + 1, BS * BS), vals.dtype)
    table = table.at[pos].set(vals)[: nrows * ncols]
    table = table.reshape(nrows, ncols, BS, BS).transpose(0, 2, 1, 3)
    return table.reshape(nrows * BS, ncols * BS)


def reference(a_vals, a_pos, p_vals, p_pos):
    result = jnp.zeros((N_COL * RBC * BS, N_ROW * CBR * BS), jnp.float32)
    for layer_index in range(N_LAYER):
        for section in range(SECTIONS):
            left = jax.vmap(lambda v, p: densify(v, p, RBC, KBS))(a_vals[:, layer_index, section], a_pos[:, layer_index, section])
            left = left.reshape(N_COL * RBC * BS, KBS * BS)
            right = jax.vmap(lambda v, p: densify(v, p, KBS, CBR))(p_vals[layer_index, section], p_pos[layer_index, section])
            right = right.transpose(1, 0, 2).reshape(KBS * BS, N_ROW * CBR * BS)
            result = result + jnp.dot(left, right, preferred_element_type=jnp.float32)
    return result
```

```python
import jax
import jax.numpy as jnp
from jax import lax
from jax.experimental import pallas as pl
from jax.experimental.pallas import tpu as pltpu
from jax.sharding import PartitionSpec as P

BS = 64
RBC = 8
KBS = 16
CBR = 4
SECTIONS = 2
SLOTS = 8
NZ, NY, NX, NCORE, NL = 4, 4, 4, 2, 4
A_EMPTY = RBC * KBS
P_EMPTY = KBS * CBR
HALF = SLOTS // 2
COPIES = 160
MESH = pl.DeviceIdType.MESH


def kernel(
    a_pos, p_pos, a_ref, p_ref, out_ref,
    abuf0, abuf1, pbuf0, pbuf1, tmp, pos_a, pos_p, inv_v, inv_a, inv_p,
    even, odd, spread, panel, part, got,
    send_sem, recv_sem, local_sem,
):
    abuf, pbuf = (abuf0, abuf1), (pbuf0, pbuf1)
    row, col, lay = lax.axis_index("row"), lax.axis_index("col"), lax.axis_index("layer")
    zh, y = row // NY, row % NY
    x, core = col // NCORE, col % NCORE

    def z_of(d):
        return (zh + d + NZ) % NZ

    def y_of(d):
        return (y + d + NY) % NY

    def x_of(d):
        return (x + d + NX) % NX

    def to_z(d):
        return {"row": z_of(d) * NY + y}

    def to_y(d):
        return {"row": zh * NY + y_of(d)}

    def to_x(d):
        return {"col": x_of(d) * NCORE + core}

    to_core = {"col": x * NCORE + 1 - core}

    def to_layer(d):
        return {"layer": (lay + d) % NL}

    partners = [to_z(1), to_z(-1), to_y(1), to_y(-1), to_x(1), to_x(-1), to_core]
    partners += [to_layer(d) for d in range(1, NL)]

    barrier = pltpu.get_barrier_semaphore()
    for partner in partners:
        pl.semaphore_signal(barrier, inc=1, device_id=partner, device_id_type=MESH)

    numbers = {}
    sent = []

    def copy(name, src, dst, target):
        k = numbers.setdefault(name, len(numbers))
        return pltpu.make_async_remote_copy(
            src_ref=src, dst_ref=dst, send_sem=send_sem.at[k], recv_sem=recv_sem.at[k],
            device_id=target, device_id_type=MESH,
        )

    def send(name, ref, target):
        c = copy(name, ref, ref, target)
        c.start()
        sent.append(c)

    def arrive(name, ref):
        copy(name, ref, ref, to_core).wait_recv()

    def a_half(s, zi, yi, h):
        return abuf[s].at[pl.ds((zi * NY + yi) * SLOTS + h * HALF, HALF)]

    def p_half(s, xi, ci, h):
        return pbuf[s].at[pl.ds((xi * NCORE + ci) * SLOTS + h * HALF, HALF)]

    def p_run(s, xi, ci):
        return pbuf[s].at[pl.ds((xi * NCORE + ci) * SLOTS, SLOTS)]

    def unfold(vals, buf, base):
        wide = vals.astype(jnp.float32)
        for j in range(32):
            tmp[pl.ds(j, SLOTS, stride=32), :] = wide[:, j * 128:(j + 1) * 128]
        for t in range(SLOTS):
            buf[base + t] = tmp[t * 32:(t + 1) * 32, :].astype(jnp.bfloat16)

    places = lax.broadcasted_iota(jnp.int32, (1, 128), 1)

    def listed(read, s, base, empty):
        line = jnp.zeros((1, 128), jnp.int32)
        for t in range(SLOTS):
            line = jnp.where(places == read(s, t), base + t - empty, line)
        return line

    unfold(a_ref[0, 0, 0], abuf0, row * SLOTS)
    unfold(a_ref[0, 0, 1], abuf1, row * SLOTS)
    unfold(p_ref[0, 0, 0], pbuf0, col * SLOTS)
    unfold(p_ref[0, 1, 0], pbuf1, col * SLOTS)
    for s in range(SECTIONS):
        pos_a[y, zh, s:s + 1, :] = listed(lambda s, t: a_pos[0, 0, s, t], s, row * SLOTS, A_EMPTY)
        pos_p[core, x, s:s + 1, :] = listed(lambda s, t: p_pos[0, s, 0, t], s, col * SLOTS, P_EMPTY)
        abuf[s][A_EMPTY] = jnp.zeros((32, 128), jnp.bfloat16)
        pbuf[s][P_EMPTY] = jnp.zeros((32, 128), jnp.bfloat16)

    pl.semaphore_wait(barrier, len(partners))

    def z_own(s):
        for up, down in ((0, 1), (1, 0)):
            send(("z", s, 1, up), a_half(s, zh, y, up), to_z(1))
            send(("z", s, -1, down), a_half(s, zh, y, down), to_z(-1))

    def z_first(s):
        arrive(("z", s, 1, 0), a_half(s, z_of(-1), y, 0))
        send(("zz", s, 0), a_half(s, z_of(-1), y, 0), to_z(1))
        arrive(("z", s, -1, 1), a_half(s, z_of(1), y, 1))
        send(("zz", s, 1), a_half(s, z_of(1), y, 1), to_z(-1))

    def y_send(s, d, h):
        ref = a_half(s, z_of(d), y, h)
        send(("y", s, d, h, 1), ref, to_y(1))
        send(("y", s, d, h, -1), ref, to_y(-1))

    def z_second(s):
        arrive(("z", s, 1, 1), a_half(s, z_of(-1), y, 1))
        y_send(s, -1, 1)
        arrive(("z", s, -1, 0), a_half(s, z_of(1), y, 0))
        y_send(s, 1, 0)

    def z_far(s):
        for h in range(2):
            arrive(("zz", s, h), a_half(s, z_of(2), y, h))
            y_send(s, 2, h)

    def y_pass(s, d, h):
        step = 1 if h == 0 else -1
        ref = a_half(s, z_of(d), y_of(-step), h)
        arrive(("y", s, d, h, step), ref)
        send(("yy", s, d, h), ref, to_y(step))

    def y_rest(s, d, h):
        step = 1 if h == 0 else -1
        arrive(("y", s, d, h, -step), a_half(s, z_of(d), y_of(step), h))
        arrive(("yy", s, d, h), a_half(s, z_of(d), y_of(2), h))

    def x_own(s):
        for up, down in ((0, 1), (1, 0)):
            send(("x", s, 1, up), p_half(s, x, core, up), to_x(1))
            send(("x", s, -1, down), p_half(s, x, core, down), to_x(-1))
        send(("c", s, 0), p_run(s, x, core), to_core)

    def x_pass(s):
        arrive(("x", s, 1, 0), p_half(s, x_of(-1), core, 0))
        send(("xx", s, 0), p_half(s, x_of(-1), core, 0), to_x(1))
        arrive(("x", s, -1, 1), p_half(s, x_of(1), core, 1))
        send(("xx", s, 1), p_half(s, x_of(1), core, 1), to_x(-1))
        arrive(("x", s, 1, 1), p_half(s, x_of(-1), core, 1))
        send(("c", s, -1), p_run(s, x_of(-1), core), to_core)
        arrive(("x", s, -1, 0), p_half(s, x_of(1), core, 0))
        send(("c", s, 1), p_run(s, x_of(1), core), to_core)

    def x_far(s):
        for h in range(2):
            arrive(("xx", s, h), p_half(s, x_of(2), core, h))
        send(("c", s, 2), p_run(s, x_of(2), core), to_core)

    def x_rest(s):
        for d in (0, -1, 1, 2):
            arrive(("c", s, d), p_run(s, x_of(d), 1 - core))

    def p_panel(s):
        for k in range(KBS):
            for m in range(CBR // 2):
                first = pbuf[s][inv_p[s, k * CBR + 2 * m]].astype(jnp.float32)
                second = pbuf[s][inv_p[s, k * CBR + 2 * m + 1]].astype(jnp.float32)
                spread[m, pl.ds(k * BS, 32, stride=2), :] = jnp.concatenate([first[:, :BS], second[:, :BS]], axis=1)
                spread[m, pl.ds(k * BS + 1, 32, stride=2), :] = jnp.concatenate([first[:, BS:], second[:, BS:]], axis=1)
        for m in range(CBR // 2):
            panel[s, :, m * 128:(m + 1) * 128] = spread[m].astype(jnp.bfloat16)

    def a_panel(s):
        for b in range(RBC):
            rows = slice(b * 32, (b + 1) * 32)
            for m in range(KBS // 2):
                first = abuf[s][inv_a[s, b * KBS + 2 * m]]
                second = abuf[s][inv_a[s, b * KBS + 2 * m + 1]]
                lanes = slice(m * 128, (m + 1) * 128)
                even[rows, lanes] = jnp.concatenate([first[:, :BS], second[:, :BS]], axis=1)
                odd[rows, lanes] = jnp.concatenate([first[:, BS:], second[:, BS:]], axis=1)

    def multiply(s):
        for which, left in enumerate((even, odd)):
            for q in range(NL):
                term = jnp.dot(left[q * 64:(q + 1) * 64, :], panel[s], preferred_element_type=jnp.float32)
                part[q, which] = term if s == 0 else part[q, which] + term

    z_own(0)
    for h in range(2):
        y_send(0, 0, h)
    x_own(0)
    send(("pz", 1), pos_a.at[y, zh], to_z(1))
    send(("pz", -1), pos_a.at[y, zh], to_z(-1))
    send(("px", 1), pos_p.at[core, x], to_x(1))
    send(("px", -1), pos_p.at[core, x], to_x(-1))
    for h in range(2):
        y_send(1, 0, h)
    x_own(1)

    arrive(("pz", 1), pos_a.at[y, z_of(-1)])
    send(("pzz",), pos_a.at[y, z_of(-1)], to_z(1))
    arrive(("px", 1), pos_p.at[core, x_of(-1)])
    send(("pxx",), pos_p.at[core, x_of(-1)], to_x(1))
    arrive(("pz", -1), pos_a.at[y, z_of(1)])
    arrive(("px", -1), pos_p.at[core, x_of(1)])

    x_pass(0)
    for h in range(2):
        y_pass(0, 0, h)
    arrive(("pzz",), pos_a.at[y, z_of(2)])
    send(("py", 1), pos_a.at[y], to_y(1))
    send(("py", -1), pos_a.at[y], to_y(-1))
    arrive(("pxx",), pos_p.at[core, x_of(2)])
    send(("pc",), pos_p.at[core], to_core)

    z_first(0)
    z_own(1)
    y_send(0, -1, 0)
    y_send(0, 1, 1)
    x_far(0)
    x_pass(1)
    for h in range(2):
        y_pass(1, 0, h)
    arrive(("py", 1), pos_a.at[y_of(-1)])
    send(("pyy",), pos_a.at[y_of(-1)], to_y(1))
    z_second(0)
    y_pass(0, -1, 0)
    y_pass(0, 1, 1)
    x_far(1)

    arrive(("pc",), pos_p.at[1 - core])
    arrive(("py", -1), pos_a.at[y_of(1)])
    arrive(("pyy",), pos_a.at[y_of(2)])
    inv_v[0] = jnp.clip(P_EMPTY + jnp.sum(jnp.sum(pos_p[...], axis=0), axis=0), 0, P_EMPTY)
    inv_v[1] = jnp.clip(A_EMPTY + jnp.sum(jnp.sum(pos_a[...], axis=0), axis=0), 0, A_EMPTY)
    to_p = pltpu.make_async_copy(inv_v.at[0], inv_p, local_sem.at[0])
    to_a = pltpu.make_async_copy(inv_v.at[1], inv_a, local_sem.at[1])
    to_p.start()
    to_a.start()

    y_pass(0, -1, 1)
    y_pass(0, 1, 0)
    z_far(0)
    to_p.wait()
    to_a.wait()
    x_rest(0)
    p_panel(0)
    z_first(1)
    y_send(1, -1, 0)
    y_send(1, 1, 1)
    for h in range(2):
        y_pass(0, 2, h)
    x_rest(1)
    p_panel(1)
    y_pass(1, -1, 0)
    y_pass(1, 1, 1)
    z_second(1)
    for d in (0, -1, 1, 2):
        for h in range(2):
            y_rest(0, d, h)
    a_panel(0)
    multiply(0)
    y_pass(1, -1, 1)
    y_pass(1, 1, 0)
    z_far(1)
    for h in range(2):
        y_pass(1, 2, h)
    for d in (0, -1, 1, 2):
        for h in range(2):
            y_rest(1, d, h)
    a_panel(1)
    multiply(1)

    for d in (2, 1, 3):
        quarter = (lay + d) % NL
        c = copy(("r", d), part.at[quarter], got.at[d - 1], to_layer(d))
        c.start()
        sent.append(c)
    for c in sent:
        c.wait_send()
    for d in (1, 3, 2):
        arrive(("r", d), got.at[d - 1])
    for which in range(2):
        total = part[lay, which] + got[0, which] + got[2, which] + got[1, which]
        for m in range(CBR // 2):
            spread[m, pl.ds(which, 64, stride=2), :] = total[:, m * 128:(m + 1) * 128]
    for m in range(CBR // 2):
        out_ref[:, m * 128:(m + 1) * 128] = spread[m, :RBC * BS // NL]


def local(a_vals, a_pos, p_vals, p_pos):
    vmem, smem = pltpu.VMEM, pltpu.SMEM
    bf16, f32, i32 = jnp.bfloat16, jnp.float32, jnp.int32
    return pl.pallas_call(
        kernel,
        out_shape=jax.ShapeDtypeStruct((RBC * BS // NL, CBR * BS), f32),
        in_specs=[
            pl.BlockSpec(memory_space=smem), pl.BlockSpec(memory_space=smem),
            pl.BlockSpec(memory_space=vmem), pl.BlockSpec(memory_space=vmem),
        ],
        out_specs=pl.BlockSpec(memory_space=vmem),
        scratch_shapes=[
            vmem((A_EMPTY + 1, 32, 128), bf16),
            vmem((A_EMPTY + 1, 32, 128), bf16),
            vmem((P_EMPTY + 1, 32, 128), bf16),
            vmem((P_EMPTY + 1, 32, 128), bf16),
            vmem((SLOTS * 32, 128), f32),
            vmem((NY, NZ, SECTIONS, 128), i32),
            vmem((NCORE, NX, SECTIONS, 128), i32),
            vmem((2, SECTIONS, 128), i32),
            smem((SECTIONS, 128), i32),
            smem((SECTIONS, 128), i32),
            vmem((RBC * 32, KBS * BS), bf16),
            vmem((RBC * 32, KBS * BS), bf16),
            vmem((CBR // 2, KBS * BS, 128), f32),
            vmem((SECTIONS, KBS * BS, CBR * BS), bf16),
            vmem((NL, 2, 64, CBR * BS), f32),
            vmem((NL - 1, 2, 64, CBR * BS), f32),
            pltpu.SemaphoreType.DMA((COPIES,)),
            pltpu.SemaphoreType.DMA((COPIES,)),
            pltpu.SemaphoreType.DMA((2,)),
        ],
        compiler_params=pltpu.CompilerParams(
            collective_id=0, has_side_effects=True, vmem_limit_bytes=40 * 1024 * 1024
        ),
        name="galerkin",
    )(a_pos, p_pos, a_vals, p_vals)


def solution(mesh):
    return jax.shard_map(
        local,
        mesh=mesh,
        in_specs=(
            P("col", "layer", None, "row", None),
            P("col", "layer", None, "row"),
            P("layer", None, "row", "col", None),
            P("layer", None, "row", "col"),
        ),
        out_specs=P(("col", "layer"), "row"),
        check_vma=False,
    )
```

```python
import jax
import jax.numpy as jnp
from jax import lax
from jax.experimental import pallas as pl
from jax.experimental.pallas import tpu as pltpu
from jax.sharding import PartitionSpec as P

BS = 64
RBC = 8
KBS = 16
CBR = 4
SECTIONS = 2
SLOTS = 8
NZ, NY, NX, NCORE, NL = 4, 4, 4, 2, 4
A_EMPTY = RBC * KBS
P_EMPTY = KBS * CBR
SENT = SLOTS - 1
EXTRA = NZ * NY * SENT
ZERO = EXTRA + 1
UP = (((0, 4),), ((0, 2), (2, 1)))
DOWN = (((4, 3),), ((3, 2), (5, 2)))
HALVES = (((0, 4), (4, 3)), ((0, 3), (3, 4)))
CODES = 32767.0
SMALLEST = 1.2e-38
COPIES = 200
MESH = pl.DeviceIdType.MESH


def kernel(
    a_pos_hbm, p_pos_hbm, a_hbm, p_hbm, out_ref,
    a_pos, p_pos, a_ref, p_ref,
    abuf0, abuf1, pbuf0, pbuf1, tmp, pos_a, pos_p, inv_v, inv_a, inv_p,
    last_own, last_y, last_z, last_all,
    even, odd, spread, panel, part, code, scale, got_code, got_scale,
    send_sem, recv_sem, local_sem,
):
    abuf, pbuf = (abuf0, abuf1), (pbuf0, pbuf1)
    row, col, lay = lax.axis_index("row"), lax.axis_index("col"), lax.axis_index("layer")
    zh, y = row // NY, row % NY
    x, core = col // NCORE, col % NCORE
    bf16, f32 = jnp.bfloat16, jnp.float32

    def z_of(d):
        return (zh + d + NZ) % NZ

    def y_of(d):
        return (y + d + NY) % NY

    def x_of(d):
        return (x + d + NX) % NX

    def to_z(d):
        return {"row": z_of(d) * NY + y}

    def to_y(d):
        return {"row": zh * NY + y_of(d)}

    def to_x(d, other):
        return {"col": x_of(d) * NCORE + (1 - core if other else core)}

    def to_layer(d):
        return {"layer": (lay + d) % NL}

    ROUND = (2, 1, -1)
    CROSS = [(d, other) for d in ROUND for other in (0, 1)] + [(0, 1)]
    partners = [to_z(1), to_z(-1)] + [to_y(d) for d in ROUND]
    partners += [to_x(d, other) for d, other in CROSS] + [to_layer(d) for d in range(1, NL)]

    barrier = pltpu.get_barrier_semaphore()
    for partner in partners:
        pl.semaphore_signal(barrier, inc=1, device_id=partner, device_id_type=MESH)

    loads = [
        pltpu.make_async_copy(src, dst, local_sem.at[k])
        for k, (src, dst) in enumerate(((a_pos_hbm, a_pos), (a_hbm, a_ref), (p_hbm, p_ref), (p_pos_hbm, p_pos)))
    ]
    for load in loads:
        load.start()

    numbers = {}
    sent = []

    def copy(name, src, dst, target):
        k = numbers.setdefault(name, len(numbers))
        return pltpu.make_async_remote_copy(
            src_ref=src, dst_ref=dst, send_sem=send_sem.at[k], recv_sem=recv_sem.at[k],
            device_id=target, device_id_type=MESH,
        )

    def send(name, src, target, dst=None):
        c = copy(name, src, src if dst is None else dst, target)
        c.start()
        sent.append(c)

    def arrive(name, ref):
        copy(name, ref, ref, to_z(1)).wait_recv()

    def a_cut(s, zi, yi, cut):
        return abuf[s].at[pl.ds((zi * NY + yi) * SENT + cut[0], cut[1])]

    def p_run(s, xi, ci):
        return pbuf[s].at[pl.ds((xi * NCORE + ci) * SLOTS, SLOTS)]

    def unfold(vals):
        wide = vals.astype(f32)
        for j in range(32):
            tmp[pl.ds(j, SLOTS, stride=32), :] = wide[:, j * 128:(j + 1) * 128]

    def unfolded(t):
        return tmp[t * 32:(t + 1) * 32, :].astype(bf16)

    places = lax.broadcasted_iota(jnp.int32, (1, 128), 1)

    def listed(read, base, sent_slots, empty):
        line = jnp.zeros((1, 128), jnp.int32)
        for t in range(SLOTS):
            line = jnp.where(places == read(t), (base + t if t < sent_slots else EXTRA) - empty, line)
        return line

    nothing = jnp.zeros((32, 128), bf16)
    loads[0].wait()
    for s in range(SECTIONS):
        pos_a[y, zh, s:s + 1, :] = listed(lambda t: a_pos[0, 0, s, t], row * SENT, SENT, ZERO)
        abuf[s][ZERO] = nothing
        pbuf[s][P_EMPTY] = nothing
    loads[1].wait()
    for s in range(SECTIONS):
        unfold(a_ref[0, 0, s])
        for t in range(SENT):
            abuf[s][row * SENT + t] = unfolded(t)
        last = jnp.where(a_pos[0, 0, s, SENT] < A_EMPTY, tmp[SENT * 32:, :], 0.0).astype(bf16)
        last_own[2 * s] = last[:16]
        last_own[2 * s + 1] = last[16:]
    loads[2].wait()
    loads[3].wait()
    for s in range(SECTIONS):
        unfold(p_ref[0, s, 0])
        for t in range(SLOTS):
            pbuf[s][col * SLOTS + t] = unfolded(t)
        pos_p[col, s:s + 1, :] = listed(lambda t: p_pos[0, s, 0, t], col * SLOTS, SLOTS, P_EMPTY)

    pl.semaphore_wait(barrier, len(partners))

    def z_own(s):
        for up, down in zip(UP[s] + DOWN[s], DOWN[s] + UP[s]):
            send(("z", s, 1, up), a_cut(s, zh, y, up), to_z(1))
            send(("z", s, -1, down), a_cut(s, zh, y, down), to_z(-1))

    def z_first(s, onward):
        for up, down in zip(UP[s], DOWN[s]):
            arrive(("z", s, 1, up), a_cut(s, z_of(-1), y, up))
            send(("zz", s, up), a_cut(s, z_of(-1), y, up), to_z(1))
            arrive(("z", s, -1, down), a_cut(s, z_of(1), y, down))
            send(("zz", s, down), a_cut(s, z_of(1), y, down), to_z(-1))
            onward(s, -1, up)
            onward(s, 1, down)

    def z_second(s, onward):
        for up, down in zip(UP[s], DOWN[s]):
            arrive(("z", s, 1, down), a_cut(s, z_of(-1), y, down))
            onward(s, -1, down)
            arrive(("z", s, -1, up), a_cut(s, z_of(1), y, up))
            onward(s, 1, up)

    def z_far(s, onward):
        for pair in zip(UP[s], DOWN[s]):
            for cut in pair:
                arrive(("zz", s, cut), a_cut(s, z_of(2), y, cut))
                onward(s, 2, cut)

    def y_near(s, d, cut):
        for e in (1, -1):
            send(("y", s, d, cut, e), a_cut(s, z_of(d), y, cut), to_y(e))

    def y_step(s, cut):
        return 1 if cut == HALVES[s][0] else -1

    def y_pass(s, d, cut):
        step = y_step(s, cut)
        ref = a_cut(s, z_of(d), y_of(-step), cut)
        arrive(("y", s, d, cut, step), ref)
        send(("yy", s, d, cut), ref, to_y(step))

    def y_rest(s, d, cut):
        step = y_step(s, cut)
        arrive(("y", s, d, cut, -step), a_cut(s, z_of(d), y_of(step), cut))
        arrive(("yy", s, d, cut), a_cut(s, z_of(d), y_of(2), cut))

    def y_direct(s, d, cut):
        for e in ROUND:
            send(("y", s, d, cut, e), a_cut(s, z_of(d), y, cut), to_y(e))

    def y_arrive(s, d, cut):
        for e in ROUND:
            arrive(("y", s, d, cut, e), a_cut(s, z_of(d), y_of(-e), cut))

    def x_own(s):
        for d, other in CROSS:
            send(("x", s, d, other), p_run(s, x, core), to_x(d, other))

    def x_all(s):
        for d, other in CROSS:
            arrive(("x", s, d, other), p_run(s, x_of(-d), 1 - core if other else core))

    def p_panel(s):
        for k in range(KBS):
            for m in range(CBR // 2):
                first = pbuf[s][inv_p[s, k * CBR + 2 * m]].astype(f32)
                second = pbuf[s][inv_p[s, k * CBR + 2 * m + 1]].astype(f32)
                spread[m, pl.ds(k * BS, 32, stride=2), :] = jnp.concatenate([first[:, :BS], second[:, :BS]], axis=1)
                spread[m, pl.ds(k * BS + 1, 32, stride=2), :] = jnp.concatenate([first[:, BS:], second[:, BS:]], axis=1)
        for m in range(CBR // 2):
            panel[s, :, m * 128:(m + 1) * 128] = spread[m].astype(bf16)

    def a_panel(s):
        for b in range(RBC):
            rows = slice(b * 32, (b + 1) * 32)
            for m in range(KBS // 2):
                first = abuf[s][inv_a[s, b * KBS + 2 * m]]
                second = abuf[s][inv_a[s, b * KBS + 2 * m + 1]]
                lanes = slice(m * 128, (m + 1) * 128)
                even[rows, lanes] = jnp.concatenate([first[:, :BS], second[:, :BS]], axis=1)
                odd[rows, lanes] = jnp.concatenate([first[:, BS:], second[:, BS:]], axis=1)

    def product(s, q, which):
        left = (even, odd)[which][pl.ds(pl.multiple_of(q * 64, 64), 64), :]
        return jnp.dot(left, panel[s], preferred_element_type=f32)

    for d in (1, -1):
        send(("pz", d), pos_a.at[y, zh], to_z(d))
    for e in ROUND:
        send(("ly", e), last_own.at[y_of(e)], to_y(e), last_y.at[y])
    z_own(0)
    for cut in HALVES[0]:
        y_near(0, 0, cut)
    for d, other in CROSS:
        send(("px", d, other), pos_p.at[col], to_x(d, other))
    x_own(0)
    for cut in HALVES[1]:
        y_near(1, 0, cut)
    x_own(1)

    for e in ROUND:
        arrive(("ly", e), last_y.at[y_of(-e)])
    last_z[zh] = last_own[y] + last_y[y_of(1)] + last_y[y_of(-1)] + last_y[y_of(2)]
    for d in (1, -1):
        send(("lz", d), last_z.at[zh], to_z(d))
    arrive(("pz", 1), pos_a.at[y, z_of(-1)])
    send(("pzz",), pos_a.at[y, z_of(-1)], to_z(1))
    arrive(("pz", -1), pos_a.at[y, z_of(1)])
    z_own(1)

    for s in range(SECTIONS):
        for cut in HALVES[s]:
            y_pass(s, 0, cut)
    z_first(0, y_near)
    arrive(("lz", 1), last_z.at[z_of(-1)])
    send(("lzz",), last_z.at[z_of(-1)], to_z(1))
    arrive(("lz", -1), last_z.at[z_of(1)])
    arrive(("pzz",), pos_a.at[y, z_of(2)])
    for e in ROUND:
        send(("py", e), pos_a.at[y], to_y(e))
    z_second(0, y_near)

    for d, other in CROSS:
        arrive(("px", d, other), pos_p.at[x_of(-d) * NCORE + (1 - core if other else core)])
    inv_v[0] = jnp.clip(P_EMPTY + jnp.sum(pos_p[...], axis=0), 0, P_EMPTY)
    to_p = pltpu.make_async_copy(inv_v.at[0], inv_p, local_sem.at[4])
    to_p.start()
    y_pass(0, -1, HALVES[0][0])
    y_pass(0, 1, HALVES[0][1])
    y_pass(0, -1, HALVES[0][1])
    y_pass(0, 1, HALVES[0][0])
    z_first(1, y_direct)
    for e in ROUND:
        arrive(("py", e), pos_a.at[y_of(-e)])
    inv_v[1] = jnp.clip(ZERO + jnp.sum(jnp.sum(pos_a[...], axis=0), axis=0), 0, ZERO)
    to_a = pltpu.make_async_copy(inv_v.at[1], inv_a, local_sem.at[5])
    to_a.start()
    to_p.wait()
    x_all(0)
    p_panel(0)
    z_second(1, y_direct)
    x_all(1)
    p_panel(1)
    arrive(("lzz",), last_z.at[z_of(2)])
    last_all[y] = last_z[0] + last_z[1] + last_z[2] + last_z[3]
    for e in ROUND:
        send(("la", e), last_all.at[y], to_y(e))
    z_far(0, y_direct)
    to_a.wait()
    z_far(1, y_direct)
    for e in ROUND:
        arrive(("la", e), last_all.at[y_of(-e)])
    for s in range(SECTIONS):
        abuf[s][EXTRA] = jnp.concatenate([last_all[2 * s], last_all[2 * s + 1]], axis=0)
    for d in (0, -1, 1):
        for cut in HALVES[0]:
            y_rest(0, d, cut)
    for cut in HALVES[0]:
        y_arrive(0, 2, cut)
    a_panel(0)
    for q in range(NL):
        for which in range(2):
            part[q, which] = product(0, q, which)
    for cut in HALVES[1]:
        y_rest(1, 0, cut)
    for d in (-1, 1, 2):
        for cut in UP[1] + DOWN[1]:
            y_arrive(1, d, cut)
    a_panel(1)

    for d in (2, 1, 3):
        q = (lay + d) % NL
        for which in range(2):
            term = part[q, which] + product(1, q, which)
            top = jnp.maximum(jnp.max(jnp.abs(term), axis=0, keepdims=True), SMALLEST)
            scale[d - 1, which:which + 1, :] = top * (1.0 / CODES)
            code[d - 1, which] = jnp.round(term * (1.0 / top) * CODES).astype(jnp.int32).astype(jnp.int16)
        send(("s", d), scale.at[d - 1], to_layer(d), got_scale.at[d - 1])
        send(("r", d), code.at[d - 1], to_layer(d), got_code.at[d - 1])
    for which in range(2):
        part[lay, which] += product(1, lay, which)
    for c in sent:
        c.wait_send()
    for d in (1, 3, 2):
        arrive(("s", d), got_scale.at[d - 1])
        arrive(("r", d), got_code.at[d - 1])
    for which in range(2):
        total = part[lay, which]
        for d in (1, 3, 2):
            total += got_code[d - 1, which].astype(jnp.int32).astype(f32) * got_scale[d - 1, which:which + 1, :]
        for m in range(CBR // 2):
            spread[m, pl.ds(which, 64, stride=2), :] = total[:, m * 128:(m + 1) * 128]
    for m in range(CBR // 2):
        out_ref[:, m * 128:(m + 1) * 128] = spread[m, :RBC * BS // NL]


def local(a_vals, a_pos, p_vals, p_pos):
    vmem, smem = pltpu.VMEM, pltpu.SMEM
    bf16, f32, i32 = jnp.bfloat16, jnp.float32, jnp.int32
    return pl.pallas_call(
        kernel,
        out_shape=jax.ShapeDtypeStruct((RBC * BS // NL, CBR * BS), f32),
        in_specs=[
            pl.BlockSpec(memory_space=pltpu.HBM), pl.BlockSpec(memory_space=pltpu.HBM),
            pl.BlockSpec(memory_space=pltpu.HBM), pl.BlockSpec(memory_space=pltpu.HBM),
        ],
        out_specs=pl.BlockSpec(memory_space=vmem),
        scratch_shapes=[
            smem(a_pos.shape, i32),
            smem(p_pos.shape, i32),
            vmem(a_vals.shape, bf16),
            vmem(p_vals.shape, bf16),
            vmem((ZERO + 1, 32, 128), bf16),
            vmem((ZERO + 1, 32, 128), bf16),
            vmem((P_EMPTY + 1, 32, 128), bf16),
            vmem((P_EMPTY + 1, 32, 128), bf16),
            vmem((SLOTS * 32, 128), f32),
            vmem((NY, NZ, SECTIONS, 128), i32),
            vmem((NX * NCORE, SECTIONS, 128), i32),
            vmem((2, SECTIONS, 128), i32),
            smem((SECTIONS, 128), i32),
            smem((SECTIONS, 128), i32),
            vmem((NY, 16, 128), bf16),
            vmem((NY, 16, 128), bf16),
            vmem((NZ, 16, 128), bf16),
            vmem((NY, 16, 128), bf16),
            vmem((RBC * 32, KBS * BS), bf16),
            vmem((RBC * 32, KBS * BS), bf16),
            vmem((CBR // 2, KBS * BS, 128), f32),
            vmem((SECTIONS, KBS * BS, CBR * BS), bf16),
            vmem((NL, 2, 64, CBR * BS), f32),
            vmem((NL - 1, 2, 64, CBR * BS), jnp.int16),
            vmem((NL - 1, 2, CBR * BS), f32),
            vmem((NL - 1, 2, 64, CBR * BS), jnp.int16),
            vmem((NL - 1, 2, CBR * BS), f32),
            pltpu.SemaphoreType.DMA((COPIES,)),
            pltpu.SemaphoreType.DMA((COPIES,)),
            pltpu.SemaphoreType.DMA((6,)),
        ],
        compiler_params=pltpu.CompilerParams(
            collective_id=0, has_side_effects=True, vmem_limit_bytes=60 * 1024 * 1024
        ),
        name="galerkin",
    )(a_pos, p_pos, a_vals, p_vals)


def solution(mesh):
    return jax.shard_map(
        local,
        mesh=mesh,
        in_specs=(
            P("col", "layer", None, "row", None),
            P("col", "layer", None, "row"),
            P("layer", None, "row", "col", None),
            P("layer", None, "row", "col"),
        ),
        out_specs=P(("col", "layer"), "row"),
        check_vma=False,
    )
```

```python
import jax
import jax.numpy as jnp
from jax import lax
from jax.experimental import pallas as pl
from jax.experimental.pallas import tpu as pltpu
from jax.sharding import PartitionSpec as P

BS = 64
RBC = 8
KBS = 16
CBR = 4
SECTIONS = 2
SLOTS = 8
NZ, NY, NX, NCORE, NL = 4, 4, 4, 2, 4
A_EMPTY = RBC * KBS
P_EMPTY = KBS * CBR
SENT = SLOTS - 1
EXTRA = NZ * NY * SENT
ZERO = EXTRA + 1
UP = (((0, 4),), ((0, 2), (2, 1)))
DOWN = (((4, 3),), ((3, 2), (5, 2)))
HALVES = (((0, 4), (4, 3)), ((0, 3), (3, 4)))
CODES = 32767.0
SMALLEST = 1.2e-38
ARRIVALS = 42
DEPARTURES = 12
MESH = pl.DeviceIdType.MESH


def kernel(
    a_pos_hbm, p_pos_hbm, a_hbm, p_hbm, out_ref,
    a_pos, p_pos, a_ref, p_ref,
    abuf0, abuf1, pbuf0, pbuf1, tmp, pos_a, pos_p, inv_v, inv_a, inv_p,
    last_own, last_y, last_z, last_all,
    even, odd, spread, panel, part, code, scale, got_code, got_scale, blocks,
    send_sem, recv_sem, local_sem,
):
    abuf, pbuf = (abuf0, abuf1), (pbuf0, pbuf1)
    row, col, lay = lax.axis_index("row"), lax.axis_index("col"), lax.axis_index("layer")
    zh, y = row // NY, row % NY
    x, core = col // NCORE, col % NCORE
    bf16, f32 = jnp.bfloat16, jnp.float32

    def z_of(d):
        return (zh + d + NZ) % NZ

    def y_of(d):
        return (y + d + NY) % NY

    def x_of(d):
        return (x + d + NX) % NX

    def to_z(d):
        return {"row": z_of(d) * NY + y}

    def to_y(d):
        return {"row": zh * NY + y_of(d)}

    def to_x(d, other):
        return {"col": x_of(d) * NCORE + (1 - core if other else core)}

    def to_layer(d):
        return {"layer": (lay + d) % NL}

    ROUND = (2, 1, -1)
    CROSS = [(d, other) for d in ROUND for other in (0, 1)] + [(0, 1)]
    partners = [to_z(1), to_z(-1)] + [to_y(d) for d in ROUND]
    partners += [to_x(d, other) for d, other in CROSS] + [to_layer(d) for d in range(1, NL)]

    barrier = pltpu.get_barrier_semaphore()
    for partner in partners:
        pl.semaphore_signal(barrier, inc=1, device_id=partner, device_id_type=MESH)

    loads = [
        pltpu.make_async_copy(src, dst, local_sem.at[k])
        for k, (src, dst) in enumerate(((a_pos_hbm, a_pos), (a_hbm, a_ref), (p_hbm, p_ref), (p_pos_hbm, p_pos)))
    ]
    for load in loads:
        load.start()

    arrivals, departures = {}, {}

    def note(groups, group, units, like):
        number, total, _ = groups.get(group, (len(groups), 0, like))
        groups[group] = (number, total + units, like)
        return number

    def gauge(group):
        _, units, like = group
        return like.at[pl.ds(0, units)]

    def send(group, out, src, target, dst=None, units=1, like=None):
        like = blocks if like is None else like
        pltpu.make_async_remote_copy(
            src_ref=src, dst_ref=src if dst is None else dst,
            send_sem=send_sem.at[note(departures, out, units, like)],
            recv_sem=recv_sem.at[note(arrivals, group, units, like)],
            device_id=target, device_id_type=MESH,
        ).start()

    def arrive(group):
        ref = gauge(arrivals[group])
        pltpu.make_async_remote_copy(
            src_ref=ref, dst_ref=ref, send_sem=send_sem.at[0], recv_sem=recv_sem.at[arrivals[group][0]],
            device_id=to_z(1), device_id_type=MESH,
        ).wait_recv()

    def depart():
        for group in departures.values():
            ref = gauge(group)
            pltpu.make_async_remote_copy(
                src_ref=ref, dst_ref=ref, send_sem=send_sem.at[group[0]], recv_sem=recv_sem.at[0],
                device_id=to_z(1), device_id_type=MESH,
            ).wait_send()

    def a_cut(s, zi, yi, cut):
        return abuf[s].at[pl.ds((zi * NY + yi) * SENT + cut[0], cut[1])]

    def p_run(s, xi, ci):
        return pbuf[s].at[pl.ds((xi * NCORE + ci) * SLOTS, SLOTS)]

    def unfold(vals):
        wide = vals.astype(f32)
        for j in range(32):
            tmp[pl.ds(j, SLOTS, stride=32), :] = wide[:, j * 128:(j + 1) * 128]

    def unfolded(t):
        return tmp[t * 32:(t + 1) * 32, :].astype(bf16)

    places = lax.broadcasted_iota(jnp.int32, (1, 128), 1)

    def listed(read, base, sent_slots, empty):
        line = jnp.zeros((1, 128), jnp.int32)
        for t in range(SLOTS):
            line = jnp.where(places == read(t), (base + t if t < sent_slots else EXTRA) - empty, line)
        return line

    nothing = jnp.zeros((32, 128), bf16)
    loads[0].wait()
    for s in range(SECTIONS):
        pos_a[y, zh, s:s + 1, :] = listed(lambda t: a_pos[0, 0, s, t], row * SENT, SENT, ZERO)
        abuf[s][ZERO] = nothing
        pbuf[s][P_EMPTY] = nothing
    loads[1].wait()
    for s in range(SECTIONS):
        unfold(a_ref[0, 0, s])
        for t in range(SENT):
            abuf[s][row * SENT + t] = unfolded(t)
        last = jnp.where(a_pos[0, 0, s, SENT] < A_EMPTY, tmp[SENT * 32:, :], 0.0).astype(bf16)
        last_own[2 * s] = last[:16]
        last_own[2 * s + 1] = last[16:]
    loads[2].wait()
    loads[3].wait()
    for s in range(SECTIONS):
        unfold(p_ref[0, s, 0])
        for t in range(SLOTS):
            pbuf[s][col * SLOTS + t] = unfolded(t)
        pos_p[col, s:s + 1, :] = listed(lambda t: p_pos[0, s, 0, t], col * SLOTS, SLOTS, P_EMPTY)

    pl.semaphore_wait(barrier, len(partners))

    def z_send(group, s, zi, cut, d):
        send(group, "z", a_cut(s, zi, y, cut), to_z(d), units=cut[1])

    def z_own(s):
        for up, down in zip(UP[s] + DOWN[s], DOWN[s] + UP[s]):
            z_send(("z", s, 1, up), s, zh, up, 1)
            z_send(("z", s, -1, down), s, zh, down, -1)

    def z_first(s, onward):
        for up, down in zip(UP[s], DOWN[s]):
            arrive(("z", s, 1, up))
            z_send(("zz", s, up), s, z_of(-1), up, 1)
            arrive(("z", s, -1, down))
            z_send(("zz", s, down), s, z_of(1), down, -1)
            onward(s, -1, up)
            onward(s, 1, down)

    def z_second(s, onward):
        for up, down in zip(UP[s], DOWN[s]):
            arrive(("z", s, 1, down))
            onward(s, -1, down)
            arrive(("z", s, -1, up))
            onward(s, 1, up)

    def z_far(s, onward):
        for pair in zip(UP[s], DOWN[s]):
            for cut in pair:
                arrive(("zz", s, cut))
                onward(s, 2, cut)

    def y_send(group, s, zi, yi, cut, e):
        send(group, ("y", s), a_cut(s, zi, yi, cut), to_y(e), units=cut[1])

    def y_step(s, cut):
        return 1 if cut == HALVES[s][0] else -1

    def y_near(s, d, cut):
        step = y_step(s, cut)
        y_send(("y", s, d, cut), s, z_of(d), y, cut, step)
        y_send(("y", s), s, z_of(d), y, cut, -step)

    def y_pass(s, d, cut):
        step = y_step(s, cut)
        arrive(("y", s, d, cut))
        y_send(("y", s), s, z_of(d), y_of(-step), cut, step)

    def y_direct(s, d, cut):
        for e in ROUND:
            y_send(("y", s), s, z_of(d), y, cut, e)

    def x_own(s):
        for d, other in CROSS:
            send(("x", s), "x", p_run(s, x, core), to_x(d, other), units=SLOTS)

    def p_panel(s):
        for k in range(KBS):
            for m in range(CBR // 2):
                first = pbuf[s][inv_p[s, k * CBR + 2 * m]].astype(f32)
                second = pbuf[s][inv_p[s, k * CBR + 2 * m + 1]].astype(f32)
                spread[m, pl.ds(k * BS, 32, stride=2), :] = jnp.concatenate([first[:, :BS], second[:, :BS]], axis=1)
                spread[m, pl.ds(k * BS + 1, 32, stride=2), :] = jnp.concatenate([first[:, BS:], second[:, BS:]], axis=1)
        for m in range(CBR // 2):
            panel[s, :, m * 128:(m + 1) * 128] = spread[m].astype(bf16)

    def a_panel(s):
        for b in range(RBC):
            rows = slice(b * 32, (b + 1) * 32)
            for m in range(KBS // 2):
                first = abuf[s][inv_a[s, b * KBS + 2 * m]]
                second = abuf[s][inv_a[s, b * KBS + 2 * m + 1]]
                lanes = slice(m * 128, (m + 1) * 128)
                even[rows, lanes] = jnp.concatenate([first[:, :BS], second[:, :BS]], axis=1)
                odd[rows, lanes] = jnp.concatenate([first[:, BS:], second[:, BS:]], axis=1)

    def product(s, q, which):
        left = (even, odd)[which][pl.ds(pl.multiple_of(q * 64, 64), 64), :]
        return jnp.dot(left, panel[s], preferred_element_type=f32)

    for d in (1, -1):
        send(("pz", d), "pz", pos_a.at[y, zh], to_z(d), like=pos_a.at[0])
    for e in ROUND:
        send("ly", "ly", last_own.at[y_of(e)], to_y(e), last_y.at[y], like=last_y)
    z_own(0)
    for cut in HALVES[0]:
        y_near(0, 0, cut)
    for d, other in CROSS:
        send("px", "px", pos_p.at[col], to_x(d, other), like=pos_p)
    x_own(0)
    for cut in HALVES[1]:
        y_near(1, 0, cut)
    x_own(1)

    arrive("ly")
    last_z[zh] = last_own[y] + last_y[y_of(1)] + last_y[y_of(-1)] + last_y[y_of(2)]
    for d in (1, -1):
        send(("lz", d), "lz", last_z.at[zh], to_z(d), like=last_z)
    arrive(("pz", 1))
    send("pzz", "pz", pos_a.at[y, z_of(-1)], to_z(1), like=pos_a.at[0])
    arrive(("pz", -1))
    z_own(1)

    for s in range(SECTIONS):
        for cut in HALVES[s]:
            y_pass(s, 0, cut)
    z_first(0, y_near)
    arrive(("lz", 1))
    send("lzz", "lz", last_z.at[z_of(-1)], to_z(1), like=last_z)
    arrive(("lz", -1))
    arrive("pzz")
    for e in ROUND:
        send("py", "py", pos_a.at[y], to_y(e), like=pos_a)
    z_second(0, y_near)

    arrive("px")
    inv_v[0] = jnp.clip(P_EMPTY + jnp.sum(pos_p[...], axis=0), 0, P_EMPTY)
    to_p = pltpu.make_async_copy(inv_v.at[0], inv_p, local_sem.at[4])
    to_p.start()
    y_pass(0, -1, HALVES[0][0])
    y_pass(0, 1, HALVES[0][1])
    y_pass(0, -1, HALVES[0][1])
    y_pass(0, 1, HALVES[0][0])
    z_first(1, y_direct)
    arrive("py")
    inv_v[1] = jnp.clip(ZERO + jnp.sum(jnp.sum(pos_a[...], axis=0), axis=0), 0, ZERO)
    to_a = pltpu.make_async_copy(inv_v.at[1], inv_a, local_sem.at[5])
    to_a.start()
    to_p.wait()
    arrive(("x", 0))
    p_panel(0)
    z_second(1, y_direct)
    arrive(("x", 1))
    p_panel(1)
    arrive("lzz")
    last_all[y] = last_z[0] + last_z[1] + last_z[2] + last_z[3]
    for e in ROUND:
        send("la", "la", last_all.at[y], to_y(e), like=last_all)
    z_far(0, y_direct)
    to_a.wait()
    z_far(1, y_direct)
    arrive("la")
    for s in range(SECTIONS):
        abuf[s][EXTRA] = jnp.concatenate([last_all[2 * s], last_all[2 * s + 1]], axis=0)
    arrive(("y", 0))
    a_panel(0)
    for q in range(NL):
        for which in range(2):
            part[q, which] = product(0, q, which)
    arrive(("y", 1))
    a_panel(1)

    for d in (2, 1, 3):
        q = (lay + d) % NL
        for which in range(2):
            term = part[q, which] + product(1, q, which)
            top = jnp.maximum(jnp.max(jnp.abs(term), axis=0, keepdims=True), SMALLEST)
            scale[d - 1, which:which + 1, :] = top * (1.0 / CODES)
            code[d - 1, which] = jnp.round(term * (1.0 / top) * CODES).astype(jnp.int32).astype(jnp.int16)
        send("s", "s", scale.at[d - 1], to_layer(d), got_scale.at[d - 1], like=scale)
        send("r", "r", code.at[d - 1], to_layer(d), got_code.at[d - 1], like=code)
    for which in range(2):
        part[lay, which] += product(1, lay, which)
    depart()
    arrive("s")
    arrive("r")
    assert len(arrivals) <= ARRIVALS and len(departures) <= DEPARTURES
    for which in range(2):
        total = part[lay, which]
        for d in (1, 3, 2):
            total += got_code[d - 1, which].astype(jnp.int32).astype(f32) * got_scale[d - 1, which:which + 1, :]
        for m in range(CBR // 2):
            spread[m, pl.ds(which, 64, stride=2), :] = total[:, m * 128:(m + 1) * 128]
    for m in range(CBR // 2):
        out_ref[:, m * 128:(m + 1) * 128] = spread[m, :RBC * BS // NL]


def local(a_vals, a_pos, p_vals, p_pos):
    vmem, smem = pltpu.VMEM, pltpu.SMEM
    bf16, f32, i32 = jnp.bfloat16, jnp.float32, jnp.int32
    return pl.pallas_call(
        kernel,
        out_shape=jax.ShapeDtypeStruct((RBC * BS // NL, CBR * BS), f32),
        in_specs=[
            pl.BlockSpec(memory_space=pl.ANY), pl.BlockSpec(memory_space=pl.ANY),
            pl.BlockSpec(memory_space=pl.ANY), pl.BlockSpec(memory_space=pl.ANY),
        ],
        out_specs=pl.BlockSpec(memory_space=vmem),
        scratch_shapes=[
            smem(a_pos.shape, i32),
            smem(p_pos.shape, i32),
            vmem(a_vals.shape, bf16),
            vmem(p_vals.shape, bf16),
            vmem((ZERO + 1, 32, 128), bf16),
            vmem((ZERO + 1, 32, 128), bf16),
            vmem((P_EMPTY + 1, 32, 128), bf16),
            vmem((P_EMPTY + 1, 32, 128), bf16),
            vmem((SLOTS * 32, 128), f32),
            vmem((NY, NZ, SECTIONS, 128), i32),
            vmem((NX * NCORE, SECTIONS, 128), i32),
            vmem((2, SECTIONS, 128), i32),
            smem((SECTIONS, 128), i32),
            smem((SECTIONS, 128), i32),
            vmem((NY, 16, 128), bf16),
            vmem((NY, 16, 128), bf16),
            vmem((NZ, 16, 128), bf16),
            vmem((NY, 16, 128), bf16),
            vmem((RBC * 32, KBS * BS), bf16),
            vmem((RBC * 32, KBS * BS), bf16),
            vmem((CBR // 2, KBS * BS, 128), f32),
            vmem((SECTIONS, KBS * BS, CBR * BS), bf16),
            vmem((NL, 2, 64, CBR * BS), f32),
            vmem((NL - 1, 2, 64, CBR * BS), jnp.int16),
            vmem((NL - 1, 2, CBR * BS), f32),
            vmem((NL - 1, 2, 64, CBR * BS), jnp.int16),
            vmem((NL - 1, 2, CBR * BS), f32),
            vmem((A_EMPTY, 32, 128), bf16),
            pltpu.SemaphoreType.DMA((DEPARTURES,)),
            pltpu.SemaphoreType.DMA((ARRIVALS,)),
            pltpu.SemaphoreType.DMA((6,)),
        ],
        compiler_params=pltpu.CompilerParams(
            collective_id=0, has_side_effects=True, vmem_limit_bytes=40 * 1024 * 1024
        ),
        name="galerkin",
    )(*(pltpu.with_memory_space_constraint(array, pltpu.HBM) for array in (a_pos, p_pos, a_vals, p_vals)))


def solution(mesh):
    return jax.shard_map(
        local,
        mesh=mesh,
        in_specs=(
            P("col", "layer", None, "row", None),
            P("col", "layer", None, "row"),
            P("layer", None, "row", "col", None),
            P("layer", None, "row", "col"),
        ),
        out_specs=P(("col", "layer"), "row"),
        check_vma=False,
    )
```

```python
import jax
import jax.numpy as jnp
from jax import lax
from jax.experimental import pallas as pl
from jax.experimental.pallas import tpu as pltpu
from jax.sharding import PartitionSpec as P

BS = 64
RBC = 8
KBS = 16
CBR = 4
SECTIONS = 2
SLOTS = 8
NZ, NY, NX, NCORE, NL = 4, 4, 4, 2, 4
A_EMPTY = RBC * KBS
P_EMPTY = KBS * CBR
SENT = SLOTS - 1
EXTRA = NZ * NY * SENT
ZERO = EXTRA + 1
HALVES = (((0, 4), (4, 3)), ((0, 3), (3, 4)))
UP = (((0, 2), (2, 2)), ((0, 2), (2, 1)))
DOWN = (((4, 2), (6, 1)), ((3, 2), (5, 2)))
CODES = 32767.0
SMALLEST = 1.2e-38
ARRIVALS = 44
DEPARTURES = 12
MESH = pl.DeviceIdType.MESH


def kernel(
    a_pos_hbm, p_pos_hbm, a_hbm, p_hbm, out_ref,
    a_pos, p_pos, a_ref, p_ref,
    abuf0, abuf1, pbuf0, pbuf1, tmp, pos_a, pos_p, inv_v, inv_a, inv_p,
    last_own, last_y, last_z, last_all,
    even, odd, spread, panel, part, code, scale, got_code, got_scale, blocks,
    send_sem, recv_sem, local_sem,
):
    abuf, pbuf = (abuf0, abuf1), (pbuf0, pbuf1)
    row, col, lay = lax.axis_index("row"), lax.axis_index("col"), lax.axis_index("layer")
    zh, y = row // NY, row % NY
    x, core = col // NCORE, col % NCORE
    bf16, f32 = jnp.bfloat16, jnp.float32

    def z_of(d):
        return (zh + d + NZ) % NZ

    def y_of(d):
        return (y + d + NY) % NY

    def x_of(d):
        return (x + d + NX) % NX

    def to_z(d):
        return {"row": z_of(d) * NY + y}

    def to_y(d):
        return {"row": zh * NY + y_of(d)}

    def to_x(d, other):
        return {"col": x_of(d) * NCORE + (1 - core if other else core)}

    owners = ((lay + 2) % NL, (lay + 1) % NL, (lay + 3) % NL)

    ROUND = (2, 1, -1)
    CROSS = [(d, other) for d in ROUND for other in (0, 1)] + [(0, 1)]
    partners = [to_z(1), to_z(-1)] + [to_y(d) for d in ROUND]
    partners += [to_x(d, other) for d, other in CROSS] + [{"layer": q} for q in owners]

    barrier = pltpu.get_barrier_semaphore()
    for partner in partners:
        pl.semaphore_signal(barrier, inc=1, device_id=partner, device_id_type=MESH)

    loads = [
        pltpu.make_async_copy(src, dst, local_sem.at[k])
        for k, (src, dst) in enumerate(((a_pos_hbm, a_pos), (a_hbm, a_ref), (p_hbm, p_ref), (p_pos_hbm, p_pos)))
    ]
    for load in loads:
        load.start()

    arrivals, departures = {}, {}

    def note(groups, group, units, like):
        number, total, _ = groups.get(group, (len(groups), 0, like))
        groups[group] = (number, total + units, like)
        return number

    def gauge(group):
        _, units, like = group
        return like.at[pl.ds(0, units)]

    def send(group, out, src, target, dst=None, units=1, like=None):
        like = blocks if like is None else like
        pltpu.make_async_remote_copy(
            src_ref=src, dst_ref=src if dst is None else dst,
            send_sem=send_sem.at[note(departures, out, units, like)],
            recv_sem=recv_sem.at[note(arrivals, group, units, like)],
            device_id=target, device_id_type=MESH,
        ).start()

    def arrive(group):
        ref = gauge(arrivals[group])
        pltpu.make_async_remote_copy(
            src_ref=ref, dst_ref=ref, send_sem=send_sem.at[0], recv_sem=recv_sem.at[arrivals[group][0]],
            device_id=to_z(1), device_id_type=MESH,
        ).wait_recv()

    def depart():
        for group in departures.values():
            ref = gauge(group)
            pltpu.make_async_remote_copy(
                src_ref=ref, dst_ref=ref, send_sem=send_sem.at[group[0]], recv_sem=recv_sem.at[0],
                device_id=to_z(1), device_id_type=MESH,
            ).wait_send()

    def a_cut(s, zi, yi, cut):
        return abuf[s].at[pl.ds((zi * NY + yi) * SENT + cut[0], cut[1])]

    def p_run(s, xi, ci):
        return pbuf[s].at[pl.ds((xi * NCORE + ci) * SLOTS, SLOTS)]

    def unfold(vals):
        wide = vals.astype(f32)
        for j in range(32):
            tmp[pl.ds(j, SLOTS, stride=32), :] = wide[:, j * 128:(j + 1) * 128]

    def unfolded(t):
        return tmp[t * 32:(t + 1) * 32, :].astype(bf16)

    places = lax.broadcasted_iota(jnp.int32, (1, 128), 1)

    def listed(read, base, sent_slots, empty):
        line = jnp.zeros((1, 128), jnp.int32)
        for t in range(SLOTS):
            line = jnp.where(places == read(t), (base + t if t < sent_slots else EXTRA) - empty, line)
        return line

    nothing = jnp.zeros((32, 128), bf16)
    loads[0].wait()
    for s in range(SECTIONS):
        pos_a[y, zh, s:s + 1, :] = listed(lambda t: a_pos[0, 0, s, t], row * SENT, SENT, ZERO)
        abuf[s][ZERO] = nothing
        pbuf[s][P_EMPTY] = nothing
    loads[1].wait()
    for s in range(SECTIONS):
        unfold(a_ref[0, 0, s])
        for t in range(SENT):
            abuf[s][row * SENT + t] = unfolded(t)
        last = jnp.where(a_pos[0, 0, s, SENT] < A_EMPTY, tmp[SENT * 32:, :], 0.0).astype(bf16)
        last_own[2 * s] = last[:16]
        last_own[2 * s + 1] = last[16:]
    loads[2].wait()
    loads[3].wait()
    for s in range(SECTIONS):
        unfold(p_ref[0, s, 0])
        for t in range(SLOTS):
            pbuf[s][col * SLOTS + t] = unfolded(t)
        pos_p[col, s:s + 1, :] = listed(lambda t: p_pos[0, s, 0, t], col * SLOTS, SLOTS, P_EMPTY)

    pl.semaphore_wait(barrier, len(partners))

    def z_send(group, s, zi, cut, d):
        send(group, "z", a_cut(s, zi, y, cut), to_z(d), units=cut[1])

    def z_own(s):
        up, down = HALVES[s]
        for rising, falling in ((up, down), (down, up)):
            z_send(("z", s, 1, rising), s, zh, rising, 1)
            z_send(("z", s, -1, falling), s, zh, falling, -1)

    def z_first(s):
        up, down = HALVES[s]
        arrive(("z", s, 1, up))
        for cut in UP[s]:
            z_send(("zz", s, cut), s, z_of(-1), cut, 1)
        arrive(("z", s, -1, down))
        for cut in DOWN[s]:
            z_send(("zz", s, cut), s, z_of(1), cut, -1)
        y_near(s, -1, up)
        y_near(s, 1, down)

    def z_second(s):
        up, down = HALVES[s]
        arrive(("z", s, 1, down))
        y_near(s, -1, down)
        arrive(("z", s, -1, up))
        y_near(s, 1, up)

    def z_far(s):
        for pair in zip(UP[s], DOWN[s]):
            for cut in pair:
                arrive(("zz", s, cut))
                y_direct(s, 2, cut)

    def y_send(group, s, zi, yi, cut, e):
        send(group, ("y", s), a_cut(s, zi, yi, cut), to_y(e), units=cut[1])

    def y_step(s, cut):
        return 1 if cut == HALVES[s][0] else -1

    def y_near(s, d, cut):
        step = y_step(s, cut)
        y_send(("y", s, d, cut), s, z_of(d), y, cut, step)
        y_send(("y", s), s, z_of(d), y, cut, -step)

    def y_pass(s, d, cut):
        step = y_step(s, cut)
        arrive(("y", s, d, cut))
        y_send(("y", s), s, z_of(d), y_of(-step), cut, step)

    def y_direct(s, d, cut):
        for e in ROUND:
            y_send(("y", s), s, z_of(d), y, cut, e)

    def x_own(s):
        for d, other in CROSS:
            send(("x", s), "x", p_run(s, x, core), to_x(d, other), units=SLOTS)

    def p_panel(s):
        for k in range(KBS):
            for m in range(CBR // 2):
                first = pbuf[s][inv_p[s, k * CBR + 2 * m]].astype(f32)
                second = pbuf[s][inv_p[s, k * CBR + 2 * m + 1]].astype(f32)
                spread[m, pl.ds(k * BS, 32, stride=2), :] = jnp.concatenate([first[:, :BS], second[:, :BS]], axis=1)
                spread[m, pl.ds(k * BS + 1, 32, stride=2), :] = jnp.concatenate([first[:, BS:], second[:, BS:]], axis=1)
        for m in range(CBR // 2):
            panel[s, :, m * 128:(m + 1) * 128] = spread[m].astype(bf16)

    def a_panel(s):
        for b in range(RBC):
            rows = slice(b * 32, (b + 1) * 32)
            for m in range(KBS // 2):
                first = abuf[s][inv_a[s, b * KBS + 2 * m]]
                second = abuf[s][inv_a[s, b * KBS + 2 * m + 1]]
                lanes = slice(m * 128, (m + 1) * 128)
                even[rows, lanes] = jnp.concatenate([first[:, :BS], second[:, :BS]], axis=1)
                odd[rows, lanes] = jnp.concatenate([first[:, BS:], second[:, BS:]], axis=1)

    def product(s, q, which):
        left = (even, odd)[which][pl.ds(pl.multiple_of(q * 64, 64), 64), :]
        return jnp.dot(left, panel[s], preferred_element_type=f32)

    for d in (1, -1):
        send(("pz", d), "pz", pos_a.at[y, zh], to_z(d), like=pos_a.at[0])
    z_own(0)
    for e in ROUND:
        send("ly", "ly", last_own.at[y_of(e)], to_y(e), last_y.at[y], like=last_y)
    for cut in HALVES[0]:
        y_near(0, 0, cut)
    for d, other in CROSS:
        send("px", "px", pos_p.at[col], to_x(d, other), like=pos_p)
    x_own(0)
    for cut in HALVES[1]:
        y_near(1, 0, cut)
    x_own(1)

    arrive("ly")
    last_z[zh] = last_own[y] + last_y[y_of(1)] + last_y[y_of(-1)] + last_y[y_of(2)]
    for d in (1, -1):
        send(("lz", d), "lz", last_z.at[zh], to_z(d), like=last_z)
    arrive(("pz", 1))
    send("pzz", "pz", pos_a.at[y, z_of(-1)], to_z(1), like=pos_a.at[0])
    arrive(("pz", -1))
    z_own(1)

    for s in range(SECTIONS):
        for cut in HALVES[s]:
            y_pass(s, 0, cut)
    z_first(0)
    z_second(0)
    arrive(("lz", 1))
    send("lzz", "lz", last_z.at[z_of(-1)], to_z(1), like=last_z)
    arrive(("lz", -1))
    arrive("pzz")
    for e in ROUND:
        send("py", "py", pos_a.at[y], to_y(e), like=pos_a)
    arrive("px")
    inv_v[0] = jnp.clip(P_EMPTY + jnp.sum(pos_p[...], axis=0), 0, P_EMPTY)
    to_p = pltpu.make_async_copy(inv_v.at[0], inv_p, local_sem.at[4])
    to_p.start()
    y_pass(0, -1, HALVES[0][0])
    y_pass(0, 1, HALVES[0][1])
    z_first(1)
    y_pass(0, -1, HALVES[0][1])
    y_pass(0, 1, HALVES[0][0])
    to_p.wait()
    arrive(("x", 0))
    p_panel(0)
    arrive("py")
    inv_v[1] = jnp.clip(ZERO + jnp.sum(jnp.sum(pos_a[...], axis=0), axis=0), 0, ZERO)
    to_a = pltpu.make_async_copy(inv_v.at[1], inv_a, local_sem.at[5])
    to_a.start()
    z_second(1)
    y_pass(1, -1, HALVES[1][0])
    y_pass(1, 1, HALVES[1][1])
    z_far(0)
    arrive(("x", 1))
    p_panel(1)
    arrive("lzz")
    last_all[y] = last_z[0] + last_z[1] + last_z[2] + last_z[3]
    for e in ROUND:
        send("la", "la", last_all.at[y], to_y(e), like=last_all)
    y_pass(1, -1, HALVES[1][1])
    y_pass(1, 1, HALVES[1][0])
    to_a.wait()
    z_far(1)
    arrive("la")
    for s in range(SECTIONS):
        abuf[s][EXTRA] = jnp.concatenate([last_all[2 * s], last_all[2 * s + 1]], axis=0)
    arrive(("y", 0))
    a_panel(0)
    for q in range(NL):
        for which in range(2):
            part[q, which] = product(0, q, which)
    arrive(("y", 1))
    a_panel(1)

    for k, q in enumerate(owners):
        for which in range(2):
            term = part[q, which] + product(1, q, which)
            top = jnp.maximum(jnp.max(jnp.abs(term), axis=0, keepdims=True), SMALLEST)
            scale[k, which:which + 1, :] = top * (1.0 / CODES)
            code[k, which] = jnp.round(term * (1.0 / top) * CODES).astype(jnp.int32).astype(jnp.int16)
        send("s", "s", scale.at[k], {"layer": q}, got_scale.at[k], like=scale)
        send("r", "r", code.at[k], {"layer": q}, got_code.at[k], like=code)
    for which in range(2):
        part[lay, which] += product(1, lay, which)
    depart()
    arrive("s")
    arrive("r")
    assert len(arrivals) <= ARRIVALS and len(departures) <= DEPARTURES
    for which in range(2):
        total = part[lay, which]
        for k in range(NL - 1):
            total += got_code[k, which].astype(jnp.int32).astype(f32) * got_scale[k, which:which + 1, :]
        for m in range(CBR // 2):
            spread[m, pl.ds(which, 64, stride=2), :] = total[:, m * 128:(m + 1) * 128]
    for m in range(CBR // 2):
        out_ref[:, m * 128:(m + 1) * 128] = spread[m, :RBC * BS // NL]


def local(a_vals, a_pos, p_vals, p_pos):
    vmem, smem = pltpu.VMEM, pltpu.SMEM
    bf16, f32, i32 = jnp.bfloat16, jnp.float32, jnp.int32
    return pl.pallas_call(
        kernel,
        out_shape=jax.ShapeDtypeStruct((RBC * BS // NL, CBR * BS), f32),
        in_specs=[
            pl.BlockSpec(memory_space=pl.ANY), pl.BlockSpec(memory_space=pl.ANY),
            pl.BlockSpec(memory_space=pl.ANY), pl.BlockSpec(memory_space=pl.ANY),
        ],
        out_specs=pl.BlockSpec(memory_space=vmem),
        scratch_shapes=[
            smem(a_pos.shape, i32),
            smem(p_pos.shape, i32),
            vmem(a_vals.shape, bf16),
            vmem(p_vals.shape, bf16),
            vmem((ZERO + 1, 32, 128), bf16),
            vmem((ZERO + 1, 32, 128), bf16),
            vmem((P_EMPTY + 1, 32, 128), bf16),
            vmem((P_EMPTY + 1, 32, 128), bf16),
            vmem((SLOTS * 32, 128), f32),
            vmem((NY, NZ, SECTIONS, 128), i32),
            vmem((NX * NCORE, SECTIONS, 128), i32),
            vmem((2, SECTIONS, 128), i32),
            smem((SECTIONS, 128), i32),
            smem((SECTIONS, 128), i32),
            vmem((NY, 16, 128), bf16),
            vmem((NY, 16, 128), bf16),
            vmem((NZ, 16, 128), bf16),
            vmem((NY, 16, 128), bf16),
            vmem((RBC * 32, KBS * BS), bf16),
            vmem((RBC * 32, KBS * BS), bf16),
            vmem((CBR // 2, KBS * BS, 128), f32),
            vmem((SECTIONS, KBS * BS, CBR * BS), bf16),
            vmem((NL, 2, 64, CBR * BS), f32),
            vmem((NL - 1, 2, 64, CBR * BS), jnp.int16),
            vmem((NL - 1, 2, CBR * BS), f32),
            vmem((NL - 1, 2, 64, CBR * BS), jnp.int16),
            vmem((NL - 1, 2, CBR * BS), f32),
            vmem((A_EMPTY, 32, 128), bf16),
            pltpu.SemaphoreType.DMA((DEPARTURES,)),
            pltpu.SemaphoreType.DMA((ARRIVALS,)),
            pltpu.SemaphoreType.DMA((6,)),
        ],
        compiler_params=pltpu.CompilerParams(
            collective_id=0, has_side_effects=True, vmem_limit_bytes=40 * 1024 * 1024
        ),
        name="galerkin",
    )(*(pltpu.with_memory_space_constraint(array, pltpu.HBM) for array in (a_pos, p_pos, a_vals, p_vals)))


def solution(mesh):
    return jax.shard_map(
        local,
        mesh=mesh,
        in_specs=(
            P("col", "layer", None, "row", None),
            P("col", "layer", None, "row"),
            P("layer", None, "row", "col", None),
            P("layer", None, "row", "col"),
        ),
        out_specs=P(("col", "layer"), "row"),
        check_vma=False,
    )
```

```python
import jax
import jax.numpy as jnp
from jax import lax
from jax.experimental import pallas as pl
from jax.experimental.pallas import tpu as pltpu
from jax.sharding import PartitionSpec as P

BS = 64
RBC = 8
KBS = 16
CBR = 4
SECTIONS = 2
SLOTS = 8
NZ, NY, NX, NCORE, NL = 4, 4, 4, 2, 4
A_EMPTY = RBC * KBS
P_EMPTY = KBS * CBR
SENT = SLOTS - 1
EXTRA = NZ * NY * SENT
ZERO = EXTRA + 1
HALVES = (((0, 4), (4, 3)), ((0, 3), (3, 4)))
UP = (((0, 2), (2, 2)), ((0, 2), (2, 1)))
DOWN = (((4, 2), (6, 1)), ((3, 2), (5, 2)))
CODES = 32767.0
SMALLEST = 1.2e-38
ARRIVALS = 47
DEPARTURES = 14
MESH = pl.DeviceIdType.MESH


def kernel(
    a_pos_hbm, p_pos_hbm, a_hbm, p_hbm, out_ref,
    a_pos, p_pos, a_ref, p_ref,
    abuf0, abuf1, pbuf0, pbuf1, tmp, pos_a, pos_p, inv_v, inv_a, inv_p,
    last_own, last_y, last_z, last_all,
    even, odd, spread, panel, part, code, scale, got_code, got_scale, blocks,
    send_sem, recv_sem, local_sem,
):
    abuf, pbuf = (abuf0, abuf1), (pbuf0, pbuf1)
    row, col, lay = lax.axis_index("row"), lax.axis_index("col"), lax.axis_index("layer")
    zh, y = row // NY, row % NY
    x, core = col // NCORE, col % NCORE
    bf16, f32 = jnp.bfloat16, jnp.float32

    def z_of(d):
        return (zh + d + NZ) % NZ

    def y_of(d):
        return (y + d + NY) % NY

    def x_of(d):
        return (x + d + NX) % NX

    def to_z(d):
        return {"row": z_of(d) * NY + y}

    def to_y(d):
        return {"row": zh * NY + y_of(d)}

    def to_x(d, other):
        return {"col": x_of(d) * NCORE + (1 - core if other else core)}

    owners = ((lay + 2) % NL, (lay + 1) % NL, (lay + 3) % NL)

    ROUND = (2, 1, -1)
    CROSS = [(d, other) for d in ROUND for other in (0, 1)] + [(0, 1)]
    SIDE = [(d, 0) for d in ROUND] + [(0, 1)]
    partners = [to_z(1), to_z(-1)] + [to_y(d) for d in ROUND]
    partners += [to_x(d, other) for d, other in SIDE] + [{"layer": q} for q in owners]

    barrier = pltpu.get_barrier_semaphore()
    for partner in partners:
        pl.semaphore_signal(barrier, inc=1, device_id=partner, device_id_type=MESH)

    loads = [
        pltpu.make_async_copy(src, dst, local_sem.at[k])
        for k, (src, dst) in enumerate(((a_pos_hbm, a_pos), (a_hbm, a_ref), (p_hbm, p_ref), (p_pos_hbm, p_pos)))
    ]
    for load in loads:
        load.start()

    arrivals, departures = {}, {}

    def note(groups, group, units, like):
        number, total, _ = groups.get(group, (len(groups), 0, like))
        groups[group] = (number, total + units, like)
        return number

    def gauge(group):
        _, units, like = group
        return like.at[pl.ds(0, units)]

    def send(group, out, src, target, dst=None, units=1, like=None):
        like = blocks if like is None else like
        pltpu.make_async_remote_copy(
            src_ref=src, dst_ref=src if dst is None else dst,
            send_sem=send_sem.at[note(departures, out, units, like)],
            recv_sem=recv_sem.at[note(arrivals, group, units, like)],
            device_id=target, device_id_type=MESH,
        ).start()

    def arrive(group):
        ref = gauge(arrivals[group])
        pltpu.make_async_remote_copy(
            src_ref=ref, dst_ref=ref, send_sem=send_sem.at[0], recv_sem=recv_sem.at[arrivals[group][0]],
            device_id=to_z(1), device_id_type=MESH,
        ).wait_recv()

    def depart():
        for group in departures.values():
            ref = gauge(group)
            pltpu.make_async_remote_copy(
                src_ref=ref, dst_ref=ref, send_sem=send_sem.at[group[0]], recv_sem=recv_sem.at[0],
                device_id=to_z(1), device_id_type=MESH,
            ).wait_send()

    def a_cut(s, zi, yi, cut):
        return abuf[s].at[pl.ds((zi * NY + yi) * SENT + cut[0], cut[1])]

    def p_run(s, xi, ci):
        return pbuf[s].at[pl.ds((xi * NCORE + ci) * SLOTS, SLOTS)]

    def unfold(vals):
        wide = vals.astype(f32)
        for j in range(32):
            tmp[pl.ds(j, SLOTS, stride=32), :] = wide[:, j * 128:(j + 1) * 128]

    def unfolded(t):
        return tmp[t * 32:(t + 1) * 32, :].astype(bf16)

    places = lax.broadcasted_iota(jnp.int32, (1, 128), 1)

    def listed(read, base, sent_slots, empty):
        line = jnp.zeros((1, 128), jnp.int32)
        for t in range(SLOTS):
            line = jnp.where(places == read(t), (base + t if t < sent_slots else EXTRA) - empty, line)
        return line

    nothing = jnp.zeros((32, 128), bf16)
    loads[0].wait()
    for s in range(SECTIONS):
        pos_a[y, zh, s:s + 1, :] = listed(lambda t: a_pos[0, 0, s, t], row * SENT, SENT, ZERO)
        abuf[s][ZERO] = nothing
        pbuf[s][P_EMPTY] = nothing
    loads[1].wait()
    for s in range(SECTIONS):
        unfold(a_ref[0, 0, s])
        for t in range(SENT):
            abuf[s][row * SENT + t] = unfolded(t)
        last = jnp.where(a_pos[0, 0, s, SENT] < A_EMPTY, tmp[SENT * 32:, :], 0.0).astype(bf16)
        last_own[2 * s] = last[:16]
        last_own[2 * s + 1] = last[16:]
    loads[2].wait()
    loads[3].wait()
    for s in range(SECTIONS):
        unfold(p_ref[0, s, 0])
        for t in range(SLOTS):
            pbuf[s][col * SLOTS + t] = unfolded(t)
        pos_p[core, x, s:s + 1, :] = listed(lambda t: p_pos[0, s, 0, t], col * SLOTS, SLOTS, P_EMPTY)

    pl.semaphore_wait(barrier, len(partners))

    def z_send(group, s, zi, cut, d):
        send(group, "z", a_cut(s, zi, y, cut), to_z(d), units=cut[1])

    def z_own(s):
        up, down = HALVES[s]
        for rising, falling in ((up, down), (down, up)):
            z_send(("z", s, 1, rising), s, zh, rising, 1)
            z_send(("z", s, -1, falling), s, zh, falling, -1)

    def z_first(s):
        up, down = HALVES[s]
        arrive(("z", s, 1, up))
        for cut in UP[s]:
            z_send(("zz", s, cut), s, z_of(-1), cut, 1)
        arrive(("z", s, -1, down))
        for cut in DOWN[s]:
            z_send(("zz", s, cut), s, z_of(1), cut, -1)
        y_near(s, -1, up)
        y_near(s, 1, down)

    def z_second(s):
        up, down = HALVES[s]
        arrive(("z", s, 1, down))
        y_near(s, -1, down)
        arrive(("z", s, -1, up))
        y_near(s, 1, up)

    def z_far(s):
        for pair in zip(UP[s], DOWN[s]):
            for cut in pair:
                arrive(("zz", s, cut))
                y_direct(s, 2, cut)

    def y_send(group, s, zi, yi, cut, e):
        send(group, ("y", s), a_cut(s, zi, yi, cut), to_y(e), units=cut[1])

    def y_step(s, cut):
        return 1 if cut == HALVES[s][0] else -1

    def y_near(s, d, cut):
        step = y_step(s, cut)
        y_send(("y", s, d, cut), s, z_of(d), y, cut, step)
        y_send(("y", s), s, z_of(d), y, cut, -step)

    def y_pass(s, d, cut):
        step = y_step(s, cut)
        arrive(("y", s, d, cut))
        y_send(("y", s), s, z_of(d), y_of(-step), cut, step)

    def y_direct(s, d, cut):
        for e in ROUND:
            y_send(("y", s), s, z_of(d), y, cut, e)

    def x_own(s):
        for d in ROUND:
            send(("x", s), "x", p_run(s, x, core), to_x(d, 0), units=SLOTS)
        send(("c", s), "c", p_run(s, x, core), to_x(0, 1), units=SLOTS)

    def x_pass(s):
        arrive(("x", s))
        for d in ROUND:
            send(("c", s), "c", p_run(s, x_of(d), core), to_x(0, 1), units=SLOTS)

    def p_panel(s):
        for k in range(KBS):
            for m in range(CBR // 2):
                first = pbuf[s][inv_p[s, k * CBR + 2 * m]].astype(f32)
                second = pbuf[s][inv_p[s, k * CBR + 2 * m + 1]].astype(f32)
                spread[m, pl.ds(k * BS, 32, stride=2), :] = jnp.concatenate([first[:, :BS], second[:, :BS]], axis=1)
                spread[m, pl.ds(k * BS + 1, 32, stride=2), :] = jnp.concatenate([first[:, BS:], second[:, BS:]], axis=1)
        for m in range(CBR // 2):
            panel[s, :, m * 128:(m + 1) * 128] = spread[m].astype(bf16)

    def a_panel(s):
        for b in range(RBC):
            rows = slice(b * 32, (b + 1) * 32)
            for m in range(KBS // 2):
                first = abuf[s][inv_a[s, b * KBS + 2 * m]]
                second = abuf[s][inv_a[s, b * KBS + 2 * m + 1]]
                lanes = slice(m * 128, (m + 1) * 128)
                even[rows, lanes] = jnp.concatenate([first[:, :BS], second[:, :BS]], axis=1)
                odd[rows, lanes] = jnp.concatenate([first[:, BS:], second[:, BS:]], axis=1)

    def product(s, q, which):
        left = (even, odd)[which][pl.ds(pl.multiple_of(q * 64, 64), 64), :]
        return jnp.dot(left, panel[s], preferred_element_type=f32)

    for d in (1, -1):
        send(("pz", d), "pz", pos_a.at[y, zh], to_z(d), like=pos_a.at[0])
    z_own(0)
    for e in ROUND:
        send("ly", "ly", last_own.at[y_of(e)], to_y(e), last_y.at[y], like=last_y)
    for cut in HALVES[0]:
        y_near(0, 0, cut)
    for d in ROUND:
        send("px", "px", pos_p.at[core, x], to_x(d, 0), like=pos_p.at[0])
    x_own(0)
    for cut in HALVES[1]:
        y_near(1, 0, cut)
    x_own(1)

    arrive("ly")
    last_z[zh] = last_own[y] + last_y[y_of(1)] + last_y[y_of(-1)] + last_y[y_of(2)]
    for d in (1, -1):
        send(("lz", d), "lz", last_z.at[zh], to_z(d), like=last_z)
    arrive(("pz", 1))
    send("pzz", "pz", pos_a.at[y, z_of(-1)], to_z(1), like=pos_a.at[0])
    arrive(("pz", -1))
    z_own(1)

    z_first(0)
    for s in range(SECTIONS):
        for cut in HALVES[s]:
            y_pass(s, 0, cut)
    z_second(0)
    arrive("px")
    send("pc", "pc", pos_p.at[core], to_x(0, 1), like=pos_p)
    x_pass(0)
    arrive(("lz", 1))
    send("lzz", "lz", last_z.at[z_of(-1)], to_z(1), like=last_z)
    arrive(("lz", -1))
    arrive("pzz")
    for e in ROUND:
        send("py", "py", pos_a.at[y], to_y(e), like=pos_a)
    arrive("pc")
    inv_v[0] = jnp.clip(P_EMPTY + jnp.sum(jnp.sum(pos_p[...], axis=0), axis=0), 0, P_EMPTY)
    to_p = pltpu.make_async_copy(inv_v.at[0], inv_p, local_sem.at[4])
    to_p.start()
    y_pass(0, -1, HALVES[0][0])
    y_pass(0, 1, HALVES[0][1])
    z_first(1)
    x_pass(1)
    y_pass(0, -1, HALVES[0][1])
    y_pass(0, 1, HALVES[0][0])
    to_p.wait()
    arrive(("c", 0))
    p_panel(0)
    arrive("py")
    inv_v[1] = jnp.clip(ZERO + jnp.sum(jnp.sum(pos_a[...], axis=0), axis=0), 0, ZERO)
    to_a = pltpu.make_async_copy(inv_v.at[1], inv_a, local_sem.at[5])
    to_a.start()
    z_second(1)
    y_pass(1, -1, HALVES[1][0])
    y_pass(1, 1, HALVES[1][1])
    z_far(0)
    arrive(("c", 1))
    p_panel(1)
    arrive("lzz")
    last_all[y] = last_z[0] + last_z[1] + last_z[2] + last_z[3]
    for e in ROUND:
        send("la", "la", last_all.at[y], to_y(e), like=last_all)
    y_pass(1, -1, HALVES[1][1])
    y_pass(1, 1, HALVES[1][0])
    to_a.wait()
    z_far(1)
    arrive("la")
    for s in range(SECTIONS):
        abuf[s][EXTRA] = jnp.concatenate([last_all[2 * s], last_all[2 * s + 1]], axis=0)
    arrive(("y", 0))
    a_panel(0)
    for q in range(NL):
        for which in range(2):
            part[q, which] = product(0, q, which)
    arrive(("y", 1))
    a_panel(1)

    for k, q in enumerate(owners):
        for which in range(2):
            term = part[q, which] + product(1, q, which)
            top = jnp.maximum(jnp.max(jnp.abs(term), axis=0, keepdims=True), SMALLEST)
            scale[k, which:which + 1, :] = top * (1.0 / CODES)
            code[k, which] = jnp.round(term * (1.0 / top) * CODES).astype(jnp.int32).astype(jnp.int16)
        send("s", "s", scale.at[k], {"layer": q}, got_scale.at[k], like=scale)
        send("r", "r", code.at[k], {"layer": q}, got_code.at[k], like=code)
    for which in range(2):
        part[lay, which] += product(1, lay, which)
    depart()
    arrive("s")
    arrive("r")
    assert len(arrivals) <= ARRIVALS and len(departures) <= DEPARTURES
    for which in range(2):
        total = part[lay, which]
        for k in range(NL - 1):
            total += got_code[k, which].astype(jnp.int32).astype(f32) * got_scale[k, which:which + 1, :]
        for m in range(CBR // 2):
            spread[m, pl.ds(which, 64, stride=2), :] = total[:, m * 128:(m + 1) * 128]
    for m in range(CBR // 2):
        out_ref[:, m * 128:(m + 1) * 128] = spread[m, :RBC * BS // NL]


def local(a_vals, a_pos, p_vals, p_pos):
    vmem, smem = pltpu.VMEM, pltpu.SMEM
    bf16, f32, i32 = jnp.bfloat16, jnp.float32, jnp.int32
    return pl.pallas_call(
        kernel,
        out_shape=jax.ShapeDtypeStruct((RBC * BS // NL, CBR * BS), f32),
        in_specs=[
            pl.BlockSpec(memory_space=pl.ANY), pl.BlockSpec(memory_space=pl.ANY),
            pl.BlockSpec(memory_space=pl.ANY), pl.BlockSpec(memory_space=pl.ANY),
        ],
        out_specs=pl.BlockSpec(memory_space=vmem),
        scratch_shapes=[
            smem(a_pos.shape, i32),
            smem(p_pos.shape, i32),
            vmem(a_vals.shape, bf16),
            vmem(p_vals.shape, bf16),
            vmem((ZERO + 1, 32, 128), bf16),
            vmem((ZERO + 1, 32, 128), bf16),
            vmem((P_EMPTY + 1, 32, 128), bf16),
            vmem((P_EMPTY + 1, 32, 128), bf16),
            vmem((SLOTS * 32, 128), f32),
            vmem((NY, NZ, SECTIONS, 128), i32),
            vmem((NCORE, NX, SECTIONS, 128), i32),
            vmem((2, SECTIONS, 128), i32),
            smem((SECTIONS, 128), i32),
            smem((SECTIONS, 128), i32),
            vmem((NY, 16, 128), bf16),
            vmem((NY, 16, 128), bf16),
            vmem((NZ, 16, 128), bf16),
            vmem((NY, 16, 128), bf16),
            vmem((RBC * 32, KBS * BS), bf16),
            vmem((RBC * 32, KBS * BS), bf16),
            vmem((CBR // 2, KBS * BS, 128), f32),
            vmem((SECTIONS, KBS * BS, CBR * BS), bf16),
            vmem((NL, 2, 64, CBR * BS), f32),
            vmem((NL - 1, 2, 64, CBR * BS), jnp.int16),
            vmem((NL - 1, 2, CBR * BS), f32),
            vmem((NL - 1, 2, 64, CBR * BS), jnp.int16),
            vmem((NL - 1, 2, CBR * BS), f32),
            vmem((A_EMPTY, 32, 128), bf16),
            pltpu.SemaphoreType.DMA((DEPARTURES,)),
            pltpu.SemaphoreType.DMA((ARRIVALS,)),
            pltpu.SemaphoreType.DMA((6,)),
        ],
        compiler_params=pltpu.CompilerParams(
            collective_id=0, has_side_effects=True, vmem_limit_bytes=40 * 1024 * 1024
        ),
        name="galerkin",
    )(*(pltpu.with_memory_space_constraint(array, pltpu.HBM) for array in (a_pos, p_pos, a_vals, p_vals)))


def solution(mesh):
    return jax.shard_map(
        local,
        mesh=mesh,
        in_specs=(
            P("col", "layer", None, "row", None),
            P("col", "layer", None, "row"),
            P("layer", None, "row", "col", None),
            P("layer", None, "row", "col"),
        ),
        out_specs=P(("col", "layer"), "row"),
        check_vma=False,
    )
```

```python
import jax
import jax.numpy as jnp
from jax import lax
from jax.experimental import pallas as pl
from jax.experimental.pallas import tpu as pltpu
from jax.sharding import PartitionSpec as P

BS = 64
RBC = 8
KBS = 16
CBR = 4
SECTIONS = 2
SLOTS = 8
NZ, NY, NX, NCORE, NL = 4, 4, 4, 2, 4
A_EMPTY = RBC * KBS
P_EMPTY = KBS * CBR
SENT = SLOTS - 1
EXTRA = NZ * NY * SENT
ZERO = EXTRA + 1
HALVES = (((0, 4), (4, 3)), ((0, 3), (3, 4)))
UP = (((0, 2), (2, 2)), ((0, 1), (1, 1), (2, 1)))
DOWN = (((4, 2), (6, 1)), ((3, 2), (5, 1), (6, 1)))
CODES = 32767.0
SMALLEST = 1.2e-38
ARRIVALS = 43
DEPARTURES = 12
MESH = pl.DeviceIdType.MESH


def kernel(
    a_pos_hbm, p_pos_hbm, a_hbm, p_hbm, out_ref,
    a_pos, p_pos, a_ref, p_ref,
    abuf0, abuf1, pbuf0, pbuf1, tmp, pos_a, pos_p, inv_v, inv_a, inv_p,
    last_own, last_y, last_z, last_all,
    even, odd, spread, panel, part, code, scale, got_code, got_scale, blocks,
    send_sem, recv_sem, local_sem,
):
    abuf, pbuf = (abuf0, abuf1), (pbuf0, pbuf1)
    row, col, lay = lax.axis_index("row"), lax.axis_index("col"), lax.axis_index("layer")
    zh, y = row // NY, row % NY
    x, core = col // NCORE, col % NCORE
    bf16, f32 = jnp.bfloat16, jnp.float32

    def z_of(d):
        return (zh + d + NZ) % NZ

    def y_of(d):
        return (y + d + NY) % NY

    def x_of(d):
        return (x + d + NX) % NX

    def to_z(d):
        return {"row": z_of(d) * NY + y}

    def to_y(d):
        return {"row": zh * NY + y_of(d)}

    def to_x(d, other):
        return {"col": x_of(d) * NCORE + (1 - core if other else core)}

    owners = ((lay + 2) % NL, (lay + 1) % NL, (lay + 3) % NL)

    ROUND = (2, 1, -1)
    CROSS = [(d, other) for d in ROUND for other in (0, 1)] + [(0, 1)]
    SIDE = [(d, 0) for d in ROUND] + [(0, 1)]
    partners = [to_z(1), to_z(-1)] + [to_y(d) for d in ROUND]
    partners += [to_x(d, other) for d, other in SIDE] + [{"layer": q} for q in owners]

    barrier = pltpu.get_barrier_semaphore()
    for partner in partners:
        pl.semaphore_signal(barrier, inc=1, device_id=partner, device_id_type=MESH)

    loads = [
        pltpu.make_async_copy(src, dst, local_sem.at[k])
        for k, (src, dst) in enumerate(((a_pos_hbm, a_pos), (a_hbm, a_ref), (p_hbm, p_ref), (p_pos_hbm, p_pos)))
    ]
    for load in loads:
        load.start()

    arrivals, departures = {}, {}

    def note(groups, group, units, like):
        number, total, _ = groups.get(group, (len(groups), 0, like))
        groups[group] = (number, total + units, like)
        return number

    def gauge(group):
        _, units, like = group
        return like.at[pl.ds(0, units)]

    def send(group, out, src, target, dst=None, units=1, like=None):
        like = blocks if like is None else like
        pltpu.make_async_remote_copy(
            src_ref=src, dst_ref=src if dst is None else dst,
            send_sem=send_sem.at[note(departures, out, units, like)],
            recv_sem=recv_sem.at[note(arrivals, group, units, like)],
            device_id=target, device_id_type=MESH,
        ).start()

    def arrive(group):
        ref = gauge(arrivals[group])
        pltpu.make_async_remote_copy(
            src_ref=ref, dst_ref=ref, send_sem=send_sem.at[0], recv_sem=recv_sem.at[arrivals[group][0]],
            device_id=to_z(1), device_id_type=MESH,
        ).wait_recv()

    def depart():
        for group in departures.values():
            ref = gauge(group)
            pltpu.make_async_remote_copy(
                src_ref=ref, dst_ref=ref, send_sem=send_sem.at[group[0]], recv_sem=recv_sem.at[0],
                device_id=to_z(1), device_id_type=MESH,
            ).wait_send()

    def a_cut(s, zi, yi, cut):
        return abuf[s].at[pl.ds((zi * NY + yi) * SENT + cut[0], cut[1])]

    def p_run(s, xi, ci):
        return pbuf[s].at[pl.ds((xi * NCORE + ci) * SLOTS, SLOTS)]

    def unfold(vals):
        wide = vals.astype(f32)
        for j in range(32):
            tmp[pl.ds(j, SLOTS, stride=32), :] = wide[:, j * 128:(j + 1) * 128]

    def unfolded(t):
        return tmp[t * 32:(t + 1) * 32, :].astype(bf16)

    places = lax.broadcasted_iota(jnp.int32, (1, 128), 1)

    def listed(read, base, sent_slots, empty):
        line = jnp.zeros((1, 128), jnp.int32)
        for t in range(SLOTS):
            line = jnp.where(places == read(t), (base + t if t < sent_slots else EXTRA) - empty, line)
        return line

    nothing = jnp.zeros((32, 128), bf16)
    loads[0].wait()
    for s in range(SECTIONS):
        pos_a[y, zh, s:s + 1, :] = listed(lambda t: a_pos[0, 0, s, t], row * SENT, SENT, ZERO)
        abuf[s][ZERO] = nothing
        pbuf[s][P_EMPTY] = nothing
    loads[1].wait()
    for s in range(SECTIONS):
        unfold(a_ref[0, 0, s])
        for t in range(SENT):
            abuf[s][row * SENT + t] = unfolded(t)
        last = jnp.where(a_pos[0, 0, s, SENT] < A_EMPTY, tmp[SENT * 32:, :], 0.0).astype(bf16)
        last_own[2 * s] = last[:16]
        last_own[2 * s + 1] = last[16:]
    loads[2].wait()
    loads[3].wait()
    for s in range(SECTIONS):
        unfold(p_ref[0, s, 0])
        for t in range(SLOTS):
            pbuf[s][col * SLOTS + t] = unfolded(t)
        pos_p[core, x, s:s + 1, :] = listed(lambda t: p_pos[0, s, 0, t], col * SLOTS, SLOTS, P_EMPTY)

    pl.semaphore_wait(barrier, len(partners))

    def z_send(group, s, zi, cut, d):
        send(group, ("y", 0), a_cut(s, zi, y, cut), to_z(d), units=cut[1])

    def z_own(s):
        up, down = HALVES[s]
        for rising, falling in ((up, down), (down, up)):
            z_send(("z", s, 1, rising), s, zh, rising, 1)
            z_send(("z", s, -1, falling), s, zh, falling, -1)

    def z_first(s):
        up, down = HALVES[s]
        arrive(("z", s, 1, up))
        for cut in UP[s]:
            z_send(("zz", s, cut), s, z_of(-1), cut, 1)
        arrive(("z", s, -1, down))
        for cut in DOWN[s]:
            z_send(("zz", s, cut), s, z_of(1), cut, -1)
        y_near(s, -1, up)
        y_near(s, 1, down)

    def z_second(s):
        up, down = HALVES[s]
        arrive(("z", s, 1, down))
        y_near(s, -1, down)
        arrive(("z", s, -1, up))
        y_near(s, 1, up)

    def z_far(s):
        for pair in zip(UP[s], DOWN[s]):
            for cut in pair:
                arrive(("zz", s, cut))
                y_direct(s, 2, cut)

    def y_send(group, s, zi, yi, cut, e):
        send(group, ("y", s), a_cut(s, zi, yi, cut), to_y(e), units=cut[1])

    def y_step(s, cut):
        return 1 if cut == HALVES[s][0] else -1

    def y_pair(s, d, cut):
        return ("y", s, "own" if d == 0 else "first" if (d == -1) == (cut == HALVES[s][0]) else "second")

    def y_near(s, d, cut):
        step = y_step(s, cut)
        y_send(y_pair(s, d, cut), s, z_of(d), y, cut, step)
        y_send(("y", s), s, z_of(d), y, cut, -step)

    def y_pass(s, d, cut):
        step = y_step(s, cut)
        if d == -1 or (d == 0 and cut == HALVES[s][0]):
            arrive(y_pair(s, d, cut))
        y_send(("y", s), s, z_of(d), y_of(-step), cut, step)

    def y_direct(s, d, cut):
        for e in ROUND:
            y_send(("y", s), s, z_of(d), y, cut, e)

    def x_own(s):
        for d in ROUND:
            send(("x", s), "c", p_run(s, x, core), to_x(d, 0), units=SLOTS)
        send(("c", s), "c", p_run(s, x, core), to_x(0, 1), units=SLOTS)

    def x_pass(s):
        arrive(("x", s))
        for d in ROUND:
            send(("c", s), "c", p_run(s, x_of(d), core), to_x(0, 1), units=SLOTS)

    def p_panel(s):
        for k in range(KBS):
            for m in range(CBR // 2):
                first = pbuf[s][inv_p[s, k * CBR + 2 * m]].astype(f32)
                second = pbuf[s][inv_p[s, k * CBR + 2 * m + 1]].astype(f32)
                spread[m, pl.ds(k * BS, 32, stride=2), :] = jnp.concatenate([first[:, :BS], second[:, :BS]], axis=1)
                spread[m, pl.ds(k * BS + 1, 32, stride=2), :] = jnp.concatenate([first[:, BS:], second[:, BS:]], axis=1)
        for m in range(CBR // 2):
            panel[s, :, m * 128:(m + 1) * 128] = spread[m].astype(bf16)

    def a_panel(s):
        for b in range(RBC):
            rows = slice(b * 32, (b + 1) * 32)
            for m in range(KBS // 2):
                first = abuf[s][inv_a[s, b * KBS + 2 * m]]
                second = abuf[s][inv_a[s, b * KBS + 2 * m + 1]]
                lanes = slice(m * 128, (m + 1) * 128)
                even[rows, lanes] = jnp.concatenate([first[:, :BS], second[:, :BS]], axis=1)
                odd[rows, lanes] = jnp.concatenate([first[:, BS:], second[:, BS:]], axis=1)

    def product(s, q, which):
        left = (even, odd)[which][pl.ds(pl.multiple_of(q * 64, 64), 64), :]
        return jnp.dot(left, panel[s], preferred_element_type=f32)

    for d in (1, -1):
        send(("pz", d), "pz", pos_a.at[y, zh], to_z(d), like=pos_a.at[0])
    z_own(0)
    for e in ROUND:
        send("ly", "ly", last_own.at[y_of(e)], to_y(e), last_y.at[y], like=last_y)
    for cut in HALVES[0]:
        y_near(0, 0, cut)
    for d in ROUND:
        send("px", "px", pos_p.at[core, x], to_x(d, 0), like=pos_p.at[0])
    x_own(0)
    for cut in HALVES[1]:
        y_near(1, 0, cut)
    x_own(1)

    arrive("ly")
    last_z[zh] = last_own[y] + last_y[y_of(1)] + last_y[y_of(-1)] + last_y[y_of(2)]
    for d in (1, -1):
        send(("lz", d), "lz", last_z.at[zh], to_z(d), like=last_z)
    arrive(("pz", 1))
    send("pzz", "pz", pos_a.at[y, z_of(-1)], to_z(1), like=pos_a.at[0])
    arrive(("pz", -1))
    z_own(1)

    z_first(0)
    for s in range(SECTIONS):
        for cut in HALVES[s]:
            y_pass(s, 0, cut)
    z_second(0)
    arrive("px")
    send("pc", "pc", pos_p.at[core], to_x(0, 1), like=pos_p)
    x_pass(0)
    arrive(("lz", 1))
    send("lzz", "lz", last_z.at[z_of(-1)], to_z(1), like=last_z)
    arrive(("lz", -1))
    arrive("pzz")
    for e in ROUND:
        send("py", "py", pos_a.at[y], to_y(e), like=pos_a)
    arrive("pc")
    inv_v[0] = jnp.clip(P_EMPTY + jnp.sum(jnp.sum(pos_p[...], axis=0), axis=0), 0, P_EMPTY)
    to_p = pltpu.make_async_copy(inv_v.at[0], inv_p, local_sem.at[4])
    to_p.start()
    y_pass(0, -1, HALVES[0][0])
    y_pass(0, 1, HALVES[0][1])
    z_first(1)
    x_pass(1)
    y_pass(0, -1, HALVES[0][1])
    y_pass(0, 1, HALVES[0][0])
    to_p.wait()
    arrive(("c", 0))
    p_panel(0)
    arrive("py")
    inv_v[1] = jnp.clip(ZERO + jnp.sum(jnp.sum(pos_a[...], axis=0), axis=0), 0, ZERO)
    to_a = pltpu.make_async_copy(inv_v.at[1], inv_a, local_sem.at[5])
    to_a.start()
    z_second(1)
    y_pass(1, -1, HALVES[1][0])
    y_pass(1, 1, HALVES[1][1])
    z_far(0)
    arrive(("c", 1))
    p_panel(1)
    arrive("lzz")
    last_all[y] = last_z[0] + last_z[1] + last_z[2] + last_z[3]
    for e in ROUND:
        send("la", "la", last_all.at[y], to_y(e), like=last_all)
    y_pass(1, -1, HALVES[1][1])
    y_pass(1, 1, HALVES[1][0])
    to_a.wait()
    z_far(1)
    arrive("la")
    for s in range(SECTIONS):
        abuf[s][EXTRA] = jnp.concatenate([last_all[2 * s], last_all[2 * s + 1]], axis=0)
    arrive(("y", 0))
    a_panel(0)
    for q in range(NL):
        for which in range(2):
            part[q, which] = product(0, q, which)
    arrive(("y", 1))
    a_panel(1)

    for k, q in enumerate(owners):
        for which in range(2):
            term = part[q, which] + product(1, q, which)
            top = jnp.maximum(jnp.max(jnp.abs(term), axis=0, keepdims=True), SMALLEST)
            scale[k, which:which + 1, :] = top * (1.0 / CODES)
            code[k, which] = jnp.round(term * (1.0 / top) * CODES).astype(jnp.int32).astype(jnp.int16)
        send("s", "s", scale.at[k], {"layer": q}, got_scale.at[k], like=scale)
        send("r", "r", code.at[k], {"layer": q}, got_code.at[k], like=code)
    for which in range(2):
        part[lay, which] += product(1, lay, which)
    depart()
    arrive("s")
    arrive("r")
    assert len(arrivals) <= ARRIVALS and len(departures) <= DEPARTURES
    for which in range(2):
        total = part[lay, which]
        for k in range(NL - 1):
            total += got_code[k, which].astype(jnp.int32).astype(f32) * got_scale[k, which:which + 1, :]
        for m in range(CBR // 2):
            spread[m, pl.ds(which, 64, stride=2), :] = total[:, m * 128:(m + 1) * 128]
    for m in range(CBR // 2):
        out_ref[:, m * 128:(m + 1) * 128] = spread[m, :RBC * BS // NL]


def local(a_vals, a_pos, p_vals, p_pos):
    vmem, smem = pltpu.VMEM, pltpu.SMEM
    bf16, f32, i32 = jnp.bfloat16, jnp.float32, jnp.int32
    return pl.pallas_call(
        kernel,
        out_shape=jax.ShapeDtypeStruct((RBC * BS // NL, CBR * BS), f32),
        in_specs=[
            pl.BlockSpec(memory_space=pl.ANY), pl.BlockSpec(memory_space=pl.ANY),
            pl.BlockSpec(memory_space=pl.ANY), pl.BlockSpec(memory_space=pl.ANY),
        ],
        out_specs=pl.BlockSpec(memory_space=vmem),
        scratch_shapes=[
            smem(a_pos.shape, i32),
            smem(p_pos.shape, i32),
            vmem(a_vals.shape, bf16),
            vmem(p_vals.shape, bf16),
            vmem((ZERO + 1, 32, 128), bf16),
            vmem((ZERO + 1, 32, 128), bf16),
            vmem((P_EMPTY + 1, 32, 128), bf16),
            vmem((P_EMPTY + 1, 32, 128), bf16),
            vmem((SLOTS * 32, 128), f32),
            vmem((NY, NZ, SECTIONS, 128), i32),
            vmem((NCORE, NX, SECTIONS, 128), i32),
            vmem((2, SECTIONS, 128), i32),
            smem((SECTIONS, 128), i32),
            smem((SECTIONS, 128), i32),
            vmem((NY, 16, 128), bf16),
            vmem((NY, 16, 128), bf16),
            vmem((NZ, 16, 128), bf16),
            vmem((NY, 16, 128), bf16),
            vmem((RBC * 32, KBS * BS), bf16),
            vmem((RBC * 32, KBS * BS), bf16),
            vmem((CBR // 2, KBS * BS, 128), f32),
            vmem((SECTIONS, KBS * BS, CBR * BS), bf16),
            vmem((NL, 2, 64, CBR * BS), f32),
            vmem((NL - 1, 2, 64, CBR * BS), jnp.int16),
            vmem((NL - 1, 2, CBR * BS), f32),
            vmem((NL - 1, 2, 64, CBR * BS), jnp.int16),
            vmem((NL - 1, 2, CBR * BS), f32),
            vmem((A_EMPTY, 32, 128), bf16),
            pltpu.SemaphoreType.DMA((DEPARTURES,)),
            pltpu.SemaphoreType.DMA((ARRIVALS,)),
            pltpu.SemaphoreType.DMA((6,)),
        ],
        compiler_params=pltpu.CompilerParams(
            collective_id=0, has_side_effects=True, vmem_limit_bytes=40 * 1024 * 1024
        ),
        name="galerkin",
    )(*(pltpu.with_memory_space_constraint(array, pltpu.HBM) for array in (a_pos, p_pos, a_vals, p_vals)))


def solution(mesh):
    return jax.shard_map(
        local,
        mesh=mesh,
        in_specs=(
            P("col", "layer", None, "row", None),
            P("col", "layer", None, "row"),
            P("layer", None, "row", "col", None),
            P("layer", None, "row", "col"),
        ),
        out_specs=P(("col", "layer"), "row"),
        check_vma=False,
    )
```

```python
import jax
import jax.numpy as jnp
from jax import lax
from jax.experimental import pallas as pl
from jax.experimental.pallas import tpu as pltpu
from jax.sharding import PartitionSpec as P

BS = 64
RBC = 8
KBS = 16
CBR = 4
SECTIONS = 2
SLOTS = 8
NZ, NY, NX, NCORE, NL = 4, 4, 4, 2, 4
A_EMPTY = RBC * KBS
P_EMPTY = KBS * CBR
SENT = SLOTS - 1
EXTRA = NZ * NY * SENT
ZERO = EXTRA + 1
HALVES = (((0, 4), (4, 3)), ((0, 3), (3, 4)))
UP = (((0, 2), (2, 2)), ((0, 1), (1, 1), (2, 1)))
DOWN = (((4, 2), (6, 1)), ((3, 2), (5, 1), (6, 1)))
CODES = 32767.0
SMALLEST = 1.2e-38
ARRIVALS = 43
DEPARTURES = 12
MESH = pl.DeviceIdType.MESH


def kernel(
    a_pos_hbm, p_pos_hbm, a_hbm, p_hbm, out_ref,
    a_pos, p_pos, a_ref, p_ref,
    abuf0, abuf1, pbuf0, pbuf1, tmp, pos_a, pos_p, inv_v, inv_a, inv_p,
    last_own, last_y, last_z, last_all,
    even, odd, spread, panel, part, code, scale, got_code, got_scale, blocks,
    send_sem, recv_sem, local_sem,
):
    abuf, pbuf = (abuf0, abuf1), (pbuf0, pbuf1)
    row, col, lay = lax.axis_index("row"), lax.axis_index("col"), lax.axis_index("layer")
    zh, y = row // NY, row % NY
    x, core = col // NCORE, col % NCORE
    bf16, f32 = jnp.bfloat16, jnp.float32

    def z_of(d):
        return (zh + d + NZ) % NZ

    def y_of(d):
        return (y + d + NY) % NY

    def x_of(d):
        return (x + d + NX) % NX

    def to_z(d):
        return {"row": z_of(d) * NY + y}

    def to_y(d):
        return {"row": zh * NY + y_of(d)}

    def to_x(d, other):
        return {"col": x_of(d) * NCORE + (1 - core if other else core)}

    owners = ((lay + 2) % NL, (lay + 1) % NL, (lay + 3) % NL)

    ROUND = (2, 1, -1)
    CROSS = [(d, other) for d in ROUND for other in (0, 1)] + [(0, 1)]
    SIDE = [(d, 0) for d in ROUND] + [(0, 1)]
    partners = [to_z(1), to_z(-1)] + [to_y(d) for d in ROUND]
    partners += [to_x(d, other) for d, other in SIDE] + [{"layer": q} for q in owners]

    barrier = pltpu.get_barrier_semaphore()
    for partner in partners:
        pl.semaphore_signal(barrier, inc=1, device_id=partner, device_id_type=MESH)

    loads = [
        pltpu.make_async_copy(src, dst, local_sem.at[k])
        for k, (src, dst) in enumerate(((a_pos_hbm, a_pos), (a_hbm, a_ref), (p_hbm, p_ref), (p_pos_hbm, p_pos)))
    ]
    for load in loads:
        load.start()

    arrivals, departures = {}, {}

    def note(groups, group, units, like):
        number, total, _ = groups.get(group, (len(groups), 0, like))
        groups[group] = (number, total + units, like)
        return number

    def gauge(group):
        _, units, like = group
        return like.at[pl.ds(0, units)]

    def send(group, out, src, target, dst=None, units=1, like=None):
        like = blocks if like is None else like
        pltpu.make_async_remote_copy(
            src_ref=src, dst_ref=src if dst is None else dst,
            send_sem=send_sem.at[note(departures, out, units, like)],
            recv_sem=recv_sem.at[note(arrivals, group, units, like)],
            device_id=target, device_id_type=MESH,
        ).start()

    def arrive(group):
        ref = gauge(arrivals[group])
        pltpu.make_async_remote_copy(
            src_ref=ref, dst_ref=ref, send_sem=send_sem.at[0], recv_sem=recv_sem.at[arrivals[group][0]],
            device_id=to_z(1), device_id_type=MESH,
        ).wait_recv()

    def depart():
        for group in departures.values():
            ref = gauge(group)
            pltpu.make_async_remote_copy(
                src_ref=ref, dst_ref=ref, send_sem=send_sem.at[group[0]], recv_sem=recv_sem.at[0],
                device_id=to_z(1), device_id_type=MESH,
            ).wait_send()

    def a_cut(s, zi, yi, cut):
        return abuf[s].at[pl.ds((zi * NY + yi) * SENT + cut[0], cut[1])]

    def p_run(s, xi, ci):
        return pbuf[s].at[pl.ds((xi * NCORE + ci) * SLOTS, SLOTS)]

    def unfold(vals):
        wide = vals.astype(f32)
        for j in range(32):
            tmp[pl.ds(j, SLOTS, stride=32), :] = wide[:, j * 128:(j + 1) * 128]

    def unfolded(t):
        return tmp[t * 32:(t + 1) * 32, :].astype(bf16)

    places = lax.broadcasted_iota(jnp.int32, (1, 128), 1)

    def listed(read, base, sent_slots, empty):
        line = jnp.zeros((1, 128), jnp.int32)
        for t in range(SLOTS):
            line = jnp.where(places == read(t), (base + t if t < sent_slots else EXTRA) - empty, line)
        return line

    nothing = jnp.zeros((32, 128), bf16)
    loads[0].wait()
    for s in range(SECTIONS):
        pos_a[y, zh, s:s + 1, :] = listed(lambda t: a_pos[0, 0, s, t], row * SENT, SENT, ZERO)
        abuf[s][ZERO] = nothing
        pbuf[s][P_EMPTY] = nothing
    loads[1].wait()
    for s in range(SECTIONS):
        unfold(a_ref[0, 0, s])
        for t in range(SENT):
            abuf[s][row * SENT + t] = unfolded(t)
        last = jnp.where(a_pos[0, 0, s, SENT] < A_EMPTY, tmp[SENT * 32:, :], 0.0).astype(bf16)
        last_own[2 * s] = last[:16]
        last_own[2 * s + 1] = last[16:]
    loads[2].wait()
    loads[3].wait()
    for s in range(SECTIONS):
        unfold(p_ref[0, s, 0])
        for t in range(SLOTS):
            pbuf[s][col * SLOTS + t] = unfolded(t)
        pos_p[core, x, s:s + 1, :] = listed(lambda t: p_pos[0, s, 0, t], col * SLOTS, SLOTS, P_EMPTY)

    pl.semaphore_wait(barrier, len(partners))

    def z_send(group, s, zi, cut, d):
        send(group, ("y", 0), a_cut(s, zi, y, cut), to_z(d), units=cut[1])

    def z_own(s):
        up, down = HALVES[s]
        for rising, falling in ((up, down), (down, up)):
            z_send(("z", s, 1, rising), s, zh, rising, 1)
            z_send(("z", s, -1, falling), s, zh, falling, -1)

    def z_first(s):
        up, down = HALVES[s]
        arrive(("z", s, 1, up))
        for cut in UP[s]:
            z_send(("zz", s, cut), s, z_of(-1), cut, 1)
        arrive(("z", s, -1, down))
        for cut in DOWN[s]:
            z_send(("zz", s, cut), s, z_of(1), cut, -1)
        y_near(s, -1, up)
        y_near(s, 1, down)

    def z_second(s):
        up, down = HALVES[s]
        arrive(("z", s, 1, down))
        y_near(s, -1, down)
        arrive(("z", s, -1, up))
        y_near(s, 1, up)

    def z_far(s):
        for pair in zip(UP[s], DOWN[s]):
            for cut in pair:
                arrive(("zz", s, cut))
                y_direct(s, 2, cut)

    def y_send(group, s, zi, yi, cut, e):
        send(group, ("y", s), a_cut(s, zi, yi, cut), to_y(e), units=cut[1])

    def y_step(s, cut):
        return 1 if cut == HALVES[s][0] else -1

    def y_pair(s, d, cut):
        return ("y", s, "own" if d == 0 else "first" if (d == -1) == (cut == HALVES[s][0]) else "second")

    def y_near(s, d, cut):
        step = y_step(s, cut)
        y_send(y_pair(s, d, cut), s, z_of(d), y, cut, step)
        y_send(("y", s), s, z_of(d), y, cut, -step)

    def y_pass(s, d, cut):
        step = y_step(s, cut)
        if d == -1 or (d == 0 and cut == HALVES[s][0]):
            arrive(y_pair(s, d, cut))
        y_send(("y", s), s, z_of(d), y_of(-step), cut, step)

    def y_direct(s, d, cut):
        for e in ROUND:
            y_send(("y", s), s, z_of(d), y, cut, e)

    def x_own(s):
        for d in ROUND:
            send(("x", s), "c", p_run(s, x, core), to_x(d, 0), units=SLOTS)
        send(("c", s), "c", p_run(s, x, core), to_x(0, 1), units=SLOTS)

    def x_pass(s):
        arrive(("x", s))
        for d in ROUND:
            send(("c", s), "c", p_run(s, x_of(d), core), to_x(0, 1), units=SLOTS)

    def p_panel(s):
        for k in range(KBS):
            for m in range(CBR // 2):
                first = pbuf[s][inv_p[s, k * CBR + 2 * m]].astype(f32)
                second = pbuf[s][inv_p[s, k * CBR + 2 * m + 1]].astype(f32)
                spread[m, pl.ds(k * BS, 32, stride=2), :] = jnp.concatenate([first[:, :BS], second[:, :BS]], axis=1)
                spread[m, pl.ds(k * BS + 1, 32, stride=2), :] = jnp.concatenate([first[:, BS:], second[:, BS:]], axis=1)
        for m in range(CBR // 2):
            panel[s, :, m * 128:(m + 1) * 128] = spread[m].astype(bf16)

    def a_panel(s):
        for b in range(RBC):
            rows = slice(b * 32, (b + 1) * 32)
            for m in range(KBS // 2):
                first = abuf[s][inv_a[s, b * KBS + 2 * m]]
                second = abuf[s][inv_a[s, b * KBS + 2 * m + 1]]
                lanes = slice(m * 128, (m + 1) * 128)
                even[rows, lanes] = jnp.concatenate([first[:, :BS], second[:, :BS]], axis=1)
                odd[rows, lanes] = jnp.concatenate([first[:, BS:], second[:, BS:]], axis=1)

    def product(s, q, which):
        left = (even, odd)[which][pl.ds(pl.multiple_of(q * 64, 64), 64), :]
        return jnp.dot(left, panel[s], preferred_element_type=f32)

    for d in (1, -1):
        send(("pz", d), "pz", pos_a.at[y, zh], to_z(d), like=pos_a.at[0])
    z_own(0)
    for e in ROUND:
        send("ly", "ly", last_own.at[y_of(e)], to_y(e), last_y.at[y], like=last_y)
    for cut in HALVES[0]:
        y_near(0, 0, cut)
    for d in ROUND:
        send("px", "px", pos_p.at[core, x], to_x(d, 0), like=pos_p.at[0])
    x_own(0)
    for cut in HALVES[1]:
        y_near(1, 0, cut)
    x_own(1)

    arrive("ly")
    last_z[zh] = last_own[y] + last_y[y_of(1)] + last_y[y_of(-1)] + last_y[y_of(2)]
    for d in (1, -1):
        send(("lz", d), "lz", last_z.at[zh], to_z(d), like=last_z)
    arrive(("pz", 1))
    send("pzz", "pz", pos_a.at[y, z_of(-1)], to_z(1), like=pos_a.at[0])
    arrive(("pz", -1))
    z_own(1)

    z_first(0)
    for s in range(SECTIONS):
        for cut in HALVES[s]:
            y_pass(s, 0, cut)
    z_second(0)
    arrive("px")
    send("pc", "pc", pos_p.at[core], to_x(0, 1), like=pos_p)
    x_pass(0)
    arrive(("lz", 1))
    send("lzz", "lz", last_z.at[z_of(-1)], to_z(1), like=last_z)
    arrive(("lz", -1))
    arrive("pzz")
    for e in ROUND:
        send("py", "py", pos_a.at[y], to_y(e), like=pos_a)
    arrive("pc")
    inv_v[0] = jnp.clip(P_EMPTY + jnp.sum(jnp.sum(pos_p[...], axis=0), axis=0), 0, P_EMPTY)
    to_p = pltpu.make_async_copy(inv_v.at[0], inv_p, local_sem.at[4])
    to_p.start()
    y_pass(0, -1, HALVES[0][0])
    y_pass(0, 1, HALVES[0][1])
    z_first(1)
    x_pass(1)
    y_pass(0, -1, HALVES[0][1])
    y_pass(0, 1, HALVES[0][0])
    to_p.wait()
    arrive(("c", 0))
    p_panel(0)
    arrive("py")
    inv_v[1] = jnp.clip(ZERO + jnp.sum(jnp.sum(pos_a[...], axis=0), axis=0), 0, ZERO)
    to_a = pltpu.make_async_copy(inv_v.at[1], inv_a, local_sem.at[5])
    to_a.start()
    z_second(1)
    y_pass(1, -1, HALVES[1][0])
    y_pass(1, 1, HALVES[1][1])
    arrive(("c", 1))
    p_panel(1)
    z_far(0)
    arrive("lzz")
    last_all[y] = last_z[0] + last_z[1] + last_z[2] + last_z[3]
    for e in ROUND:
        send("la", "la", last_all.at[y], to_y(e), like=last_all)
    y_pass(1, -1, HALVES[1][1])
    y_pass(1, 1, HALVES[1][0])
    to_a.wait()
    z_far(1)
    arrive("la")
    for s in range(SECTIONS):
        abuf[s][EXTRA] = jnp.concatenate([last_all[2 * s], last_all[2 * s + 1]], axis=0)
    arrive(("y", 0))
    a_panel(0)
    for q in range(NL):
        for which in range(2):
            part[q, which] = product(0, q, which)
    arrive(("y", 1))
    a_panel(1)

    for k, q in enumerate(owners):
        for which in range(2):
            term = part[q, which] + product(1, q, which)
            top = jnp.maximum(jnp.max(jnp.abs(term), axis=0, keepdims=True), SMALLEST)
            scale[k, which:which + 1, :] = top * (1.0 / CODES)
            code[k, which] = jnp.round(term * (1.0 / top) * CODES).astype(jnp.int32).astype(jnp.int16)
        send("s", "s", scale.at[k], {"layer": q}, got_scale.at[k], like=scale)
        send("r", "r", code.at[k], {"layer": q}, got_code.at[k], like=code)
    for which in range(2):
        part[lay, which] += product(1, lay, which)
    depart()
    arrive("s")
    arrive("r")
    assert len(arrivals) <= ARRIVALS and len(departures) <= DEPARTURES
    for which in range(2):
        total = part[lay, which]
        for k in range(NL - 1):
            total += got_code[k, which].astype(jnp.int32).astype(f32) * got_scale[k, which:which + 1, :]
        for m in range(CBR // 2):
            spread[m, pl.ds(which, 64, stride=2), :] = total[:, m * 128:(m + 1) * 128]
    for m in range(CBR // 2):
        out_ref[:, m * 128:(m + 1) * 128] = spread[m, :RBC * BS // NL]


def local(a_vals, a_pos, p_vals, p_pos):
    vmem, smem = pltpu.VMEM, pltpu.SMEM
    bf16, f32, i32 = jnp.bfloat16, jnp.float32, jnp.int32
    return pl.pallas_call(
        kernel,
        out_shape=jax.ShapeDtypeStruct((RBC * BS // NL, CBR * BS), f32),
        in_specs=[
            pl.BlockSpec(memory_space=pl.ANY), pl.BlockSpec(memory_space=pl.ANY),
            pl.BlockSpec(memory_space=pl.ANY), pl.BlockSpec(memory_space=pl.ANY),
        ],
        out_specs=pl.BlockSpec(memory_space=vmem),
        scratch_shapes=[
            smem(a_pos.shape, i32),
            smem(p_pos.shape, i32),
            vmem(a_vals.shape, bf16),
            vmem(p_vals.shape, bf16),
            vmem((ZERO + 1, 32, 128), bf16),
            vmem((ZERO + 1, 32, 128), bf16),
            vmem((P_EMPTY + 1, 32, 128), bf16),
            vmem((P_EMPTY + 1, 32, 128), bf16),
            vmem((SLOTS * 32, 128), f32),
            vmem((NY, NZ, SECTIONS, 128), i32),
            vmem((NCORE, NX, SECTIONS, 128), i32),
            vmem((2, SECTIONS, 128), i32),
            smem((SECTIONS, 128), i32),
            smem((SECTIONS, 128), i32),
            vmem((NY, 16, 128), bf16),
            vmem((NY, 16, 128), bf16),
            vmem((NZ, 16, 128), bf16),
            vmem((NY, 16, 128), bf16),
            vmem((RBC * 32, KBS * BS), bf16),
            vmem((RBC * 32, KBS * BS), bf16),
            vmem((CBR // 2, KBS * BS, 128), f32),
            vmem((SECTIONS, KBS * BS, CBR * BS), bf16),
            vmem((NL, 2, 64, CBR * BS), f32),
            vmem((NL - 1, 2, 64, CBR * BS), jnp.int16),
            vmem((NL - 1, 2, CBR * BS), f32),
            vmem((NL - 1, 2, 64, CBR * BS), jnp.int16),
            vmem((NL - 1, 2, CBR * BS), f32),
            vmem((A_EMPTY, 32, 128), bf16),
            pltpu.SemaphoreType.DMA((DEPARTURES,)),
            pltpu.SemaphoreType.DMA((ARRIVALS,)),
            pltpu.SemaphoreType.DMA((6,)),
        ],
        compiler_params=pltpu.CompilerParams(
            collective_id=0, has_side_effects=True, vmem_limit_bytes=40 * 1024 * 1024
        ),
        name="galerkin",
    )(*(pltpu.with_memory_space_constraint(array, pltpu.HBM) for array in (a_pos, p_pos, a_vals, p_vals)))


def solution(mesh):
    return jax.shard_map(
        local,
        mesh=mesh,
        in_specs=(
            P("col", "layer", None, "row", None),
            P("col", "layer", None, "row"),
            P("layer", None, "row", "col", None),
            P("layer", None, "row", "col"),
        ),
        out_specs=P(("col", "layer"), "row"),
        check_vma=False,
    )
```
